256 devices in a mesh: segment: 2 (over z_hi), space: 16 (over z_lo, x), chan: 8 (over y, core).
Axes of the slice: x: 4, y: 4, z: 8 (z_hi: 2, z_lo: 4; z = z_hi * 4 + z_lo), core: 2. Of those that a mesh axis runs over, the one named last changes fastest.
Arguments:
- acts: float32 [2, 1, 768, 18432], P('segment', None, 'chan', 'space'), may hold values from -6 to 6
- cotangent: float32 [1, 768, 18432], P(None, 'chan', 'space'), may hold values from -6 to 6
- w_in: float32 [2, 2, 8, 96, 96], P('segment', None, 'chan'), may hold values from -0.4375 to 0.4375
- w_out: float32 [2, 2, 8, 96, 96], P('segment', None, 'chan'), may hold values from -0.4375 to 0.4375
- b_in: float32 [2, 2, 768], P('segment', None, 'chan'), may hold values from -3 to 3
- b_out: float32 [2, 2, 768], P('segment', None, 'chan'), may hold values from -3 to 3
Outputs:
- adjoints: float32 [2, 1, 768, 18432], P('segment', None, 'chan', 'space')
- grad_w_in: float32 [2, 2, 8, 96, 96], P('segment', None, 'chan')
- grad_w_out: float32 [2, 2, 8, 96, 96], P('segment', None, 'chan')
- grad_b_in: float32 [2, 2, 768], P('segment', None, 'chan')
- grad_b_out: float32 [2, 2, 768], P('segment', None, 'chan')
The draws below stay inside these ranges and needn't reach their ends.
All inputs are finite; a program needn't handle non-finite values.
Results may differ from the reference program's by a relative error of at most 0.0059.
Values sent between devices are 32-bit elements; how exact they have to be, the bound alone decides.
No kernel may reach another device: no remote copies, remote signals or barrier semaphores. Data moves between devices by JAX's collectives and lax.ppermute only.
A program may use at most 64 MiB of HBM per device.

```python
import math
import jax
import jax.numpy as jnp
from jax import lax

H = 96
W = 192
BS = 96
M = 1
GROUPS = 8
C = 768
N_SEGMENT = 2


def steps_of(rng, extent, shards, smallest, high):
    loudness = 1.0
    for position, shards_of in shards:
        draws = jax.random.uniform(jax.random.fold_in(jax.random.fold_in(rng, 6), position), (shards_of,), jnp.float32, smallest / len(shards), high / len(shards))
        loudness = loudness * jnp.repeat(jnp.exp(draws), extent[position] // shards_of).reshape((-1,) + (1,) * (len(extent) - 1 - position))
    return loudness


def gaussian(rng, extent, spread, reach, split=(), kind=jnp.bfloat16):
    result = jax.random.normal(rng, extent, jnp.float32) * spread
    if len(split) > 0:
        result = steps_of(rng, extent, split, -0.22, 0.18) * result
    return jnp.clip(result, min=-reach, max=reach).astype(kind)


def setup_inputs(seed: int = 0) -> dict:
    keys = jax.random.split(jax.random.key(seed), 7)
    return {
        "acts": gaussian(keys[0], (N_SEGMENT, M, C, H * W), 1.0, 6.0, ((0, 2), (2, 8), (3, 16)), jnp.float32),
        "cotangent": gaussian(keys[1], (M, C, H * W), 1.0, 6.0, ((1, 8), (2, 16)), jnp.float32),
        "w_in": gaussian(keys[2], (N_SEGMENT, 2, GROUPS, BS, BS), (2 * BS) ** -0.5, 0.4375, ((0, 2), (2, 8)), jnp.float32),
        "w_out": gaussian(keys[3], (N_SEGMENT, 2, GROUPS, BS, BS), (2 * BS) ** -0.5, 0.4375, ((0, 2), (2, 8)), jnp.float32),
        "b_in": gaussian(keys[4], (N_SEGMENT, 2, C), 0.5, 3.0, ((0, 2), (2, 8)), jnp.float32),
        "b_out": gaussian(keys[5], (N_SEGMENT, 2, C), 0.5, 3.0, ((0, 2), (2, 8)), jnp.float32),
    }


exact = lax.Precision.HIGHEST
shrink = 0.3

def dft_tables(length):
    counter = jnp.arange(length, dtype=jnp.int32)
    product = counter[:, None] * counter[None, :] % length
    phase = product.astype(jnp.float32) * (2.0 * math.pi / length)
    factor = 1.0 / math.sqrt(length)
    return (jnp.cos(phase) * factor, jnp.sin(phase) * factor)

def along_width(field, dft_table):
    return jnp.einsum('chw,wv->chv', field, dft_table, precision=exact)

def along_height(dft_table, field):
    return jnp.einsum('uh,chv->cuv', dft_table, field, precision=exact)

def complex_mix(real_part, imag_part, weight, offsets):
    groups = weight.shape[1]
    group_size = weight.shape[2]
    split_shape = (groups, group_size) + real_part.shape[1:]
    real_split = real_part.reshape(split_shape)
    imag_split = imag_part.reshape(split_shape)
    out_real = jnp.einsum('giuv,gij->gjuv', real_split, weight[0], precision=exact) - jnp.einsum('giuv,gij->gjuv', imag_split, weight[1], precision=exact)
    out_imag = jnp.einsum('giuv,gij->gjuv', real_split, weight[1], precision=exact) + jnp.einsum('giuv,gij->gjuv', imag_split, weight[0], precision=exact)
    return (out_real.reshape(real_part.shape) + offsets[0][:, None, None], out_imag.reshape(real_part.shape) + offsets[1][:, None, None])

def soft_shrink(value):
    return jnp.where(value > shrink, value - shrink, jnp.where(value < -shrink, value + shrink, 0.0 * value))

def section(field, weight_one, weight_two, offset_one, offset_two):
    height, width = (field.shape[1], field.shape[2])
    cos_w, sin_w = dft_tables(width)
    cos_h, sin_h = dft_tables(height)
    spec_r = along_width(field, cos_w)
    spec_i = -along_width(field, sin_w)
    freq_r = along_height(cos_h, spec_r) + along_height(sin_h, spec_i)
    freq_i = along_height(cos_h, spec_i) - along_height(sin_h, spec_r)
    hid_r, hid_i = complex_mix(freq_r, freq_i, weight_one, offset_one)
    out_r, out_i = complex_mix(jax.nn.relu(hid_r), jax.nn.relu(hid_i), weight_two, offset_two)
    shr_r = soft_shrink(out_r)
    shr_i = soft_shrink(out_i)
    back_r = along_height(cos_h, shr_r) - along_height(sin_h, shr_i)
    back_i = along_height(cos_h, shr_i) + along_height(sin_h, shr_r)
    return field + along_width(back_r, cos_w) - along_width(back_i, sin_w)

def reference(acts, cotangent, w_in, w_out, b_in, b_out):
    segments = acts.shape[0]
    micro_count = acts.shape[1]
    channels = acts.shape[2]
    grid_shape = (channels, H, W)
    grad_one = jnp.zeros(w_in.shape, jnp.float32)
    grad_two = jnp.zeros(w_out.shape, jnp.float32)
    grad_off_one = jnp.zeros(b_in.shape, jnp.float32)
    grad_off_two = jnp.zeros(b_out.shape, jnp.float32)
    results = [[None] * micro_count for segment_idx in range(segments)]
    for micro in range(micro_count):
        upstream = cotangent[micro].reshape(grid_shape)
        for segment_idx in reversed(range(segments)):
            unused, pullback = jax.vjp(section, acts[segment_idx, micro].reshape(grid_shape), w_in[segment_idx], w_out[segment_idx], b_in[segment_idx], b_out[segment_idx])
            d_field, d_one, d_two, d_off_one, d_off_two = pullback(upstream)
            results[segment_idx][micro] = d_field.reshape(channels, H * W)
            grad_one = grad_one.at[segment_idx].add(d_one)
            grad_two = grad_two.at[segment_idx].add(d_two)
            grad_off_one = grad_off_one.at[segment_idx].add(d_off_one)
            grad_off_two = grad_off_two.at[segment_idx].add(d_off_two)
            upstream = d_field
    adjoints = jnp.stack([jnp.stack(results[segment_idx]) for segment_idx in range(segments)])
    return (adjoints, grad_one, grad_two, grad_off_one, grad_off_two)
```

```python
import math

import jax
import jax.numpy as jnp
import ml_dtypes
import numpy as np
from jax import lax
from jax.experimental import pallas as pl
from jax.experimental.pallas import tpu as pltpu
from jax.sharding import PartitionSpec as P

H = 96
W = 192
CH = 96
LANES = 128
N_SPACE = 16
N_SEG = 2
N_DEST = N_SPACE * N_SEG
ROWS = H // N_SPACE
COLS = W // 2 // N_DEST
BLOCK = 48
SHRINK = 0.3
BF16 = jnp.bfloat16
F32 = jnp.float32
VMEM_LIMIT = 40 * 1024 * 1024


def split_table(table, count):
    parts = []
    for _ in range(count):
        parts.append(table.astype(np.float32).astype(ml_dtypes.bfloat16))
        table = table - parts[-1].astype(np.float64)
    return np.stack(parts)


def dft(length):
    index = np.arange(length)
    phase = 2.0 * math.pi * (np.outer(index, index) % length) / length
    return np.cos(phase) / math.sqrt(length), np.sin(phase) / math.sqrt(length)


def width_table():
    cos_w, sin_w = dft(W)
    half = W // 2
    real, imag = cos_w[:half].copy(), -sin_w[:half].copy()
    imag[0] = cos_w[half]
    both = np.stack([real, imag])
    return both.reshape(2, N_DEST, COLS, W).transpose(0, 2, 1, 3)


def height_tables():
    cos_h, sin_h = dft(H)
    order = np.array([ROWS * p + r for r in range(ROWS) for p in range(N_SPACE)])
    cos_h, sin_h = cos_h[:, order], sin_h[:, order]
    zero = np.zeros_like(cos_h)
    plain = np.block([[cos_h, sin_h], [-sin_h, cos_h]])
    mirror = np.block([[cos_h, sin_h], [sin_h, -cos_h]])
    special = np.block([[cos_h, zero], [-sin_h, zero], [zero, cos_h], [zero, -sin_h]])
    return plain, np.stack([np.concatenate([plain, mirror]), special])


def row_pair_tables():
    table = width_table()
    flat = table.reshape(2 * COLS * N_DEST, W)
    zero = np.zeros_like(flat)
    both = np.block([[flat, zero], [zero, flat]])
    parts = []
    for part in range(2):
        one = table[part].reshape(COLS * N_DEST, W)
        none = np.zeros_like(one)
        parts.append(np.block([[one, none], [none, one]]))
    return both, np.stack(parts)


def cut(value, count):
    parts = []
    for n in range(count):
        parts.append(value.astype(BF16))
        if n < count - 1:
            value = value - parts[-1].astype(F32)
    return parts


def halves(value):
    return cut(value, 2)


def thirds(value):
    return cut(value, 3)


def product(a, b, contract, parts=2):
    dims = (contract, ((), ()))
    total = None
    for order in reversed(range(parts)):
        for n in range(order + 1):
            one = lax.dot_general(a[n], b[order - n], dims, preferred_element_type=F32)
            total = one if total is None else total + one
    return total


NN = ((1,), (0,))
NT = ((1,), (1,))
TN = ((0,), (0,))


def lane_index(rows):
    return lax.broadcasted_iota(jnp.int32, (rows, LANES), 1)


def slot(part, c, r):
    return (part * COLS + c) * ROWS + r


N_FIELD = 2 * COLS * ROWS


def pack_rows(put, count, values):
    lane = lane_index(count)
    for q in range(BLOCK):
        third, extra = divmod(q, 16)
        value = values.get(q)
        packed = values.get(BLOCK + extra)
        if value is None:
            value = jnp.zeros((count, LANES), F32)
        if packed is not None:
            value = jnp.where(lane < CH, value, pltpu.roll(packed, CH - 32 * third, 1))
        put(q, value)


def unpack_row(get, count, q):
    if q < BLOCK:
        return get(q)
    lane = lane_index(count)
    extra = q - BLOCK
    value = jnp.zeros((count, LANES), F32)
    for third in range(3):
        moved = pltpu.roll(get(extra + 16 * third), (32 * third - CH) % LANES, 1)
        value = jnp.where((lane >= 32 * third) & (lane < 32 * third + 32), moved, value)
    return value


def ahead_kernel(seg_ref, x_ref, g_ref, both_ref, part_ref, out_ref):
    segment = seg_ref[0]
    pad = jnp.zeros((LANES - CH, 2 * W), F32)
    values = {}
    both = [both_ref[n] for n in range(3)]
    part = [part_ref[n, segment] for n in range(2)]
    for j in range(ROWS // 2):
        lanes = pl.ds(2 * W * j, 2 * W)
        field = product(both, thirds(jnp.concatenate([x_ref[:, lanes], pad], axis=0)), NT, 3)
        adjoint = product(part, halves(jnp.concatenate([g_ref[:, lanes], pad], axis=0)), NT)
        for rr in range(2):
            for c in range(COLS):
                for of in range(2):
                    base = ((rr * 2 + of) * COLS + c) * N_DEST
                    values[slot(of, c, 2 * j + rr)] = field[base : base + N_DEST]
                base = (rr * COLS + c) * N_DEST
                values[N_FIELD + c * ROWS + 2 * j + rr] = adjoint[base : base + N_DEST]

    def put(q, value):
        out_ref[pl.ds(q, N_DEST, stride=BLOCK), :] = value

    pack_rows(put, N_DEST, values)


def middle_kernel(flag_ref, got_ref, w_ref, b_ref, plain_ref, plain_t_ref, first_ref, first_t_ref, out_ref, grads_ref):
    flag = flag_ref[0]
    plain = [plain_ref[n] for n in range(3)]
    plain_t = [plain_t_ref[n] for n in range(2)]
    first = [first_ref[n, flag] for n in range(3)]
    first_t = [first_t_ref[n, flag] for n in range(2)]
    scale = jnp.where(flag == 1, 1.0, 0.5).astype(F32)

    def row(source, q):
        def get(at):
            return got_ref[pl.ds(source * N_SPACE * BLOCK + at, N_SPACE, stride=BLOCK), :]

        return unpack_row(get, N_SPACE, q)

    def field_column(s, c):
        return jnp.concatenate([row(s, slot(of, c, r)) for of in range(2) for r in range(ROWS)], axis=0)

    def adjoint_column(c):
        return jnp.concatenate([row(of, N_FIELD + c * ROWS + r) for of in range(2) for r in range(ROWS)], axis=0)

    def ordinary(column):
        r, i = column[:H], column[H:]
        return [jnp.concatenate([r, i], axis=1), jnp.concatenate([r, -i], axis=1)]

    def special(column):
        return [
            jnp.concatenate([column[:H], column[H : 2 * H]], axis=1),
            jnp.concatenate([column[2 * H : 3 * H], column[3 * H :]], axis=1),
        ]

    adjoint_first = adjoint_column(0)
    head = product(first, thirds(jnp.concatenate([field_column(s, 0) for s in range(2)], axis=1)), NN, 3)
    rest = product(
        plain, thirds(jnp.concatenate([field_column(s, c) for s in range(2) for c in (1, 2)], axis=1)), NN, 3
    )
    adjoint_head = product(first, halves(adjoint_first), NN)
    adjoint_rest = product(plain, halves(jnp.concatenate([adjoint_column(c) for c in (1, 2)], axis=1)), NN)

    def block(value, n):
        return value[:, LANES * n : LANES * (n + 1)]

    weights = [thirds(w_ref[n]) for n in range(4)]

    forward = []
    for s in range(2):
        x = jnp.concatenate(
            special(block(head, s)) + ordinary(block(rest, 2 * s)) + ordinary(block(rest, 2 * s + 1)), axis=0
        )
        x = thirds(x)
        hid = product(x, weights[2 * s], NN, 3) + b_ref[2 * s : 2 * s + 1, :]
        act = thirds(jnp.maximum(hid, 0.0))
        out = product(act, weights[2 * s + 1], NN, 3) + b_ref[2 * s + 1 : 2 * s + 2, :]
        forward.append((x, hid, act, out))

    def backward(s, upstream):
        x, hid, act, out = forward[s]
        grad_out = jnp.where(jnp.abs(out) > SHRINK, upstream, 0.0)
        grad_out_halves = halves(grad_out)
        grad_hid = jnp.where(hid > 0.0, product(grad_out_halves, weights[2 * s + 1], NT), 0.0)
        grad_hid_halves = halves(grad_hid)
        grad_x = product(grad_hid_halves, weights[2 * s], NT)
        pairs = []
        for n, (left, right) in enumerate(((x, grad_hid_halves), (act, grad_out_halves))):
            full = product(left, right, TN)
            grads_ref[pl.ds((2 * n) * CH, CH), :] = full[:CH, :LANES] + full[LANES : LANES + CH, LANES:]
            grads_ref[pl.ds((2 * n + 1) * CH, CH), :] = full[:CH, LANES:] - full[LANES : LANES + CH, :LANES]
        offsets = []
        for value in (grad_hid, grad_out):
            total = jnp.sum(value, axis=0, keepdims=True)
            offsets += [total[:, :LANES], total[:, LANES:]]
        sums = []
        for c in (1, 2):
            one, two = grad_x[2 * c * H : (2 * c + 1) * H], grad_x[(2 * c + 1) * H : (2 * c + 2) * H]
            sums.append(
                jnp.concatenate([one[:, :LANES] + two[:, :LANES], one[:, LANES:] - two[:, LANES:]], axis=0)
            )
        lead = jnp.concatenate(
            [grad_x[:H, :LANES], grad_x[:H, LANES:], grad_x[H : 2 * H, :LANES], grad_x[H : 2 * H, LANES:]], axis=0
        )
        head_back = product(first_t, halves(lead), NN)
        rest_back = product(plain_t, halves(jnp.concatenate(sums, axis=1)), NN)
        return [head_back, block(rest_back, 0), block(rest_back, 1)], sums, offsets

    def emit(s, columns, offsets):
        values = {}
        for c in range(COLS):
            for of in range(2):
                for r in range(ROWS):
                    base = (of * ROWS + r) * N_SPACE
                    values[slot(of, c, r)] = columns[c][base : base + N_SPACE]
        share = 4 * CH // N_SPACE
        for j in range(share):
            values[N_FIELD + j] = grads_ref[pl.ds(j, N_SPACE, stride=share), :]
        for j in range(4):
            values[N_FIELD + share + j] = jnp.broadcast_to(offsets[j], (N_SPACE, LANES))

        def put(q, value):
            out_ref[pl.ds(s * N_SPACE * BLOCK + q, N_SPACE, stride=BLOCK), :] = value

        pack_rows(put, N_SPACE, values)

    upstream = jnp.concatenate(
        special(adjoint_head) + ordinary(block(adjoint_rest, 0)) + ordinary(block(adjoint_rest, 1)), axis=0
    )
    columns_one, sums, offsets = backward(1, upstream)
    emit(1, columns_one, offsets)

    head_next = product(first, halves(adjoint_first + scale * columns_one[0]), NN)
    upstream = jnp.concatenate(
        special(head_next)
        + ordinary(block(adjoint_rest, 0) + 0.5 * sums[0])
        + ordinary(block(adjoint_rest, 1) + 0.5 * sums[1]),
        axis=0,
    )
    columns_zero, sums, offsets = backward(0, upstream)
    emit(0, [one + zero for one, zero in zip(columns_one, columns_zero)], offsets)


def total_kernel(got_ref, share_ref, offset_ref):
    total = got_ref[pl.ds(0, BLOCK), :]
    for d in range(1, N_DEST):
        total = total + got_ref[pl.ds(d * BLOCK, BLOCK), :]
    share = 4 * CH // N_SPACE
    lane = lane_index(16)
    late = jnp.zeros((16, LANES), F32)
    for third in range(3):
        moved = pltpu.roll(total[16 * third : 16 * third + 16], (32 * third - CH) % LANES, 1)
        late = jnp.where((lane >= 32 * third) & (lane < 32 * third + 32), moved, late)
    early = BLOCK - N_FIELD
    for p in range(N_SPACE):
        share_ref[pl.ds(p * share, early), :] = total[N_FIELD:BLOCK]
        share_ref[pl.ds(p * share + early, share - early), :] = late[: share - early]
    offset_ref[...] = late[share - early : 16]


def after_kernel(got_ref, g_ref, pair_ref, out_ref):
    for j in range(ROWS // 2):
        rows = []
        for rr in range(2):
            for of in range(2):
                for c in range(COLS):
                    rows.append(got_ref[pl.ds(slot(of, c, 2 * j + rr), N_DEST, stride=BLOCK), :])
        spectrum = halves(jnp.concatenate(rows, axis=0))
        back = product(spectrum, [pair_ref[n] for n in range(2)], TN)
        lanes = pl.ds(2 * W * j, 2 * W)
        out_ref[:, lanes] = g_ref[:, lanes] + back[:CH]


def vmem(count):
    return [pl.BlockSpec(memory_space=pltpu.VMEM)] * count


def smem():
    return [pl.BlockSpec(memory_space=pltpu.SMEM)]


PARAMS = pltpu.CompilerParams(vmem_limit_bytes=VMEM_LIMIT)


def shards(acts, cotangent, w_in, w_out, b_in, b_out):
    segment = lax.axis_index("segment")
    space = lax.axis_index("space")
    everyone = ("segment", "space")
    block_input, given = acts[0, 0], cotangent[0]

    pair, part = row_pair_tables()
    plain, heads = height_tables()
    pair_parts = split_table(pair, 3)
    part_parts = split_table(part, 2)
    plain_parts = split_table(plain, 3)
    plain_t_parts = split_table(plain.T, 2)
    head_parts = split_table(heads, 3)
    head_t_parts = split_table(heads.transpose(0, 2, 1), 2)

    sent = pl.pallas_call(
        ahead_kernel,
        out_shape=jax.ShapeDtypeStruct((N_DEST * BLOCK, LANES), F32),
        in_specs=smem() + vmem(4),
        out_specs=pl.BlockSpec(memory_space=pltpu.VMEM),
        compiler_params=PARAMS,
        name="ahead",
    )(segment.astype(jnp.int32).reshape(1), block_input, given, pair_parts, part_parts)
    got = lax.all_to_all(sent.reshape(N_DEST, BLOCK, LANES), everyone, 0, 0, tiled=True)

    own_w = jnp.concatenate([w_in[0, :, 0], w_out[0, :, 0]])
    own_b = jnp.concatenate([b_in[0], b_out[0]])
    swap = [(0, 1), (1, 0)]
    other_w = lax.ppermute(own_w, "segment", swap)
    other_b = lax.ppermute(own_b, "segment", swap)
    is_zero = segment == 0
    all_w = jnp.concatenate([jnp.where(is_zero, own_w, other_w), jnp.where(is_zero, other_w, own_w)])
    all_b = jnp.concatenate([jnp.where(is_zero, own_b, other_b), jnp.where(is_zero, other_b, own_b)])
    all_w = jnp.pad(all_w, ((0, 0), (0, LANES - CH), (0, LANES - CH))).reshape(4, 2, LANES, LANES)
    w0, w1 = all_w[:, 0], all_w[:, 1]
    full_w = jnp.concatenate(
        [jnp.concatenate([w0, w1], axis=2), jnp.concatenate([-w1, w0], axis=2)], axis=1
    )
    full_b = jnp.pad(all_b, ((0, 0), (0, LANES - CH))).reshape(4, 2 * LANES)
    full_b = jnp.pad(full_b, ((0, 4), (0, 0)))

    flag = ((segment == 0) & (space == 0)).astype(jnp.int32).reshape(1)
    sent = pl.pallas_call(
        middle_kernel,
        out_shape=jax.ShapeDtypeStruct((N_DEST * BLOCK, LANES), F32),
        in_specs=smem() + vmem(7),
        out_specs=pl.BlockSpec(memory_space=pltpu.VMEM),
        scratch_shapes=[pltpu.VMEM((4 * CH, LANES), F32)],
        compiler_params=PARAMS,
        name="middle",
    )(flag, got.reshape(N_DEST * BLOCK, LANES), full_w, full_b, plain_parts, plain_t_parts, head_parts, head_t_parts)
    got = lax.all_to_all(sent.reshape(N_DEST, BLOCK, LANES), everyone, 0, 0, tiled=True)
    got = got.reshape(N_DEST * BLOCK, LANES)

    share = 4 * CH // N_SPACE
    mine, offsets = pl.pallas_call(
        total_kernel,
        out_shape=(
            jax.ShapeDtypeStruct((N_SPACE * share, LANES), F32),
            jax.ShapeDtypeStruct((4, LANES), F32),
        ),
        in_specs=vmem(1),
        out_specs=tuple(vmem(2)),
        compiler_params=PARAMS,
        name="total",
    )(got)
    whole = lax.all_to_all(mine.reshape(N_SPACE, share, LANES), "space", 0, 0, tiled=True)

    adjoint = pl.pallas_call(
        after_kernel,
        out_shape=jax.ShapeDtypeStruct((CH, ROWS * W), F32),
        in_specs=vmem(3),
        out_specs=pl.BlockSpec(memory_space=pltpu.VMEM),
        compiler_params=PARAMS,
        name="after",
    )(got, given, pair_parts[:2])

    whole = whole.reshape(4, CH, LANES)[:, :, :CH]
    offsets = offsets[:, :CH]
    return (
        adjoint[None, None],
        whole[:2].reshape(w_in.shape),
        whole[2:].reshape(w_out.shape),
        offsets[:2].reshape(b_in.shape),
        offsets[2:].reshape(b_out.shape),
    )


def solution(mesh):
    placed = (
        P("segment", None, "chan", "space"),
        P(None, "chan", "space"),
        P("segment", None, "chan", None, None),
        P("segment", None, "chan", None, None),
        P("segment", None, "chan"),
        P("segment", None, "chan"),
    )
    return jax.shard_map(
        shards,
        mesh=mesh,
        in_specs=placed,
        out_specs=(
            P("segment", None, "chan", "space"),
            P("segment", None, "chan", None, None),
            P("segment", None, "chan", None, None),
            P("segment", None, "chan"),
            P("segment", None, "chan"),
        ),
        check_vma=False,
    )
```

```python
import math

import jax
import jax.numpy as jnp
import ml_dtypes
import numpy as np
from jax import lax
from jax.experimental import pallas as pl
from jax.experimental.pallas import tpu as pltpu
from jax.sharding import PartitionSpec as P

H = 96
W = 192
CH = 96
LANES = 128
N_SPACE = 16
N_SEG = 2
N_DEST = N_SPACE * N_SEG
ROWS = H // N_SPACE
COLS = W // 2 // N_DEST
BLOCK = 48
SHRINK = 0.3
BF16 = jnp.bfloat16
F32 = jnp.float32
VMEM_LIMIT = 24 * 1024 * 1024
AHEAD_VMEM = 56 * 1024 * 1024


def split_table(table, count):
    parts = []
    for _ in range(count):
        parts.append(table.astype(np.float32).astype(ml_dtypes.bfloat16))
        table = table - parts[-1].astype(np.float64)
    return np.stack(parts)


def dft(length):
    index = np.arange(length)
    phase = 2.0 * math.pi * (np.outer(index, index) % length) / length
    return np.cos(phase) / math.sqrt(length), np.sin(phase) / math.sqrt(length)


def width_table():
    cos_w, sin_w = dft(W)
    half = W // 2
    real, imag = cos_w[:half].copy(), -sin_w[:half].copy()
    imag[0] = cos_w[half]
    both = np.stack([real, imag])
    return both.reshape(2, N_DEST, COLS, W).transpose(0, 2, 1, 3)


def height_tables():
    cos_h, sin_h = dft(H)
    order = np.array([ROWS * p + r for r in range(ROWS) for p in range(N_SPACE)])
    cos_h, sin_h = cos_h[:, order], sin_h[:, order]
    zero = np.zeros_like(cos_h)
    plain = np.block([[cos_h, sin_h], [-sin_h, cos_h]])
    mirror = np.block([[cos_h, sin_h], [sin_h, -cos_h]])
    special = np.block([[cos_h, zero], [-sin_h, zero], [zero, cos_h], [zero, -sin_h]])
    return plain, np.stack([np.concatenate([plain, mirror]), special])


def row_pair_table():
    flat = width_table().reshape(2 * COLS * N_DEST, W)
    zero = np.zeros_like(flat)
    return np.block([[flat, zero], [zero, flat]])


def cut(value, count):
    parts = []
    for n in range(count):
        parts.append(value.astype(BF16))
        if n < count - 1:
            value = value - parts[-1].astype(F32)
    return parts


def halves(value):
    return cut(value, 2)


def thirds(value):
    return cut(value, 3)


def product(a, b, contract, parts=2):
    dims = (contract, ((), ()))
    total = None
    for order in reversed(range(parts)):
        for n in range(order + 1):
            one = lax.dot_general(a[n], b[order - n], dims, preferred_element_type=F32)
            total = one if total is None else total + one
    return total


NN = ((1,), (0,))
NT = ((1,), (1,))
TN = ((0,), (0,))


def lane_index(rows):
    return lax.broadcasted_iota(jnp.int32, (rows, LANES), 1)


def slot(part, c, r):
    return (part * COLS + c) * ROWS + r


N_FIELD = 2 * COLS * ROWS
OFFSET_ROW = N_FIELD + COLS * ROWS


def pack_rows(put, count, values):
    lane = lane_index(count)
    for q in range(BLOCK):
        third, extra = divmod(q, 16)
        value = values.get(q)
        packed = values.get(BLOCK + extra)
        if value is None:
            value = jnp.zeros((count, LANES), F32)
        if packed is not None:
            value = jnp.where(lane < CH, value, pltpu.roll(packed, CH - 32 * third, 1))
        put(q, value)


def unpack_row(get, count, q):
    if q < BLOCK:
        return get(q)
    lane = lane_index(count)
    extra = q - BLOCK
    value = jnp.zeros((count, LANES), F32)
    for third in range(3):
        moved = pltpu.roll(get(extra + 16 * third), (32 * third - CH) % LANES, 1)
        value = jnp.where((lane >= 32 * third) & (lane < 32 * third + 32), moved, value)
    return value


def ahead_kernel(
    seg_ref, x_hbm, g_hbm, b_in_hbm, b_out_hbm, table_hbm, out_ref, x_ref, g_ref, b_in_ref, b_out_ref, table_ref, sems
):
    segment = seg_ref[0]
    pairs = [
        (table_hbm, table_ref),
        (x_hbm, x_ref),
        (g_hbm, g_ref),
        (b_in_hbm, b_in_ref),
        (b_out_hbm, b_out_ref),
    ]
    copies = [pltpu.make_async_copy(src, dst, sems.at[n]) for n, (src, dst) in enumerate(pairs)]
    for copy in copies:
        copy.start()
    pad = jnp.zeros((LANES - CH, W), F32)
    values = {}
    copies[0].wait()
    table = [table_ref[n].reshape(2 * COLS * N_DEST, W) for n in range(3)]
    part = [table_ref[n, segment] for n in range(2)]
    copies[1].wait()
    for r in range(ROWS):
        lanes = pl.ds(W * r, W)
        field = product(table, thirds(jnp.concatenate([x_ref[:, lanes], pad], axis=0)), NT, 3)
        for of in range(2):
            for c in range(COLS):
                base = (of * COLS + c) * N_DEST
                values[slot(of, c, r)] = field[base : base + N_DEST]
    copies[2].wait()
    for r in range(ROWS):
        lanes = pl.ds(W * r, W)
        adjoint = product(part, halves(jnp.concatenate([g_ref[:, lanes], pad], axis=0)), NT)
        for c in range(COLS):
            base = c * N_DEST
            values[N_FIELD + c * ROWS + r] = adjoint[base : base + N_DEST]
    copies[3].wait()
    copies[4].wait()
    fill = jnp.zeros((1, LANES - CH), F32)
    for n, ref in enumerate((b_in_ref, b_out_ref)):
        for of in range(2):
            one = jnp.concatenate([ref[of : of + 1, :], fill], axis=1)
            values[OFFSET_ROW + 2 * n + of] = jnp.broadcast_to(one, (N_DEST, LANES))

    def put(q, value):
        out_ref[pl.ds(q, N_DEST, stride=BLOCK), :] = value

    pack_rows(put, N_DEST, values)


def middle_kernel(flag_ref, got_ref, w_ref, plain_ref, plain_t_ref, first_ref, first_t_hbm, out_ref, grads_ref, first_t_ref, sem):
    flag = flag_ref[0]
    fetch = pltpu.make_async_copy(first_t_hbm.at[flag], first_t_ref, sem)
    fetch.start()
    plain = [plain_ref[n] for n in range(3)]
    plain_t = [plain_t_ref[n] for n in range(2)]
    first = [first_ref[n, flag] for n in range(3)]
    scale = jnp.where(flag == 1, 1.0, 0.5).astype(F32)

    def row(source, q):
        def get(at):
            return got_ref[pl.ds(source * N_SPACE * BLOCK + at, N_SPACE, stride=BLOCK), :]

        return unpack_row(get, N_SPACE, q)

    def field_column(s, c):
        return jnp.concatenate([row(s, slot(of, c, r)) for of in range(2) for r in range(ROWS)], axis=0)

    def adjoint_column(c):
        return jnp.concatenate([row(of, N_FIELD + c * ROWS + r) for of in range(2) for r in range(ROWS)], axis=0)

    def ordinary(column):
        r, i = column[:H], column[H:]
        return [jnp.concatenate([r, i], axis=1), jnp.concatenate([r, -i], axis=1)]

    def special(column):
        return [
            jnp.concatenate([column[:H], column[H : 2 * H]], axis=1),
            jnp.concatenate([column[2 * H : 3 * H], column[3 * H :]], axis=1),
        ]

    adjoint_first = adjoint_column(0)
    head = product(first, thirds(jnp.concatenate([field_column(s, 0) for s in range(2)], axis=1)), NN, 3)
    rest = product(
        plain, thirds(jnp.concatenate([field_column(s, c) for s in range(2) for c in (1, 2)], axis=1)), NN, 3
    )
    adjoint_head = product(first, halves(adjoint_first), NN)
    adjoint_rest = product(plain, halves(jnp.concatenate([adjoint_column(c) for c in (1, 2)], axis=1)), NN)

    def block(value, n):
        return value[:, LANES * n : LANES * (n + 1)]

    weights = [thirds(w_ref[n]) for n in range(4)]

    def offset(s, n):
        def get(at):
            return got_ref[pl.ds(s * N_SPACE * BLOCK + at, 1), :]

        return jnp.concatenate([unpack_row(get, 1, OFFSET_ROW + 2 * n + of) for of in range(2)], axis=1)

    forward = []
    for s in range(2):
        x = jnp.concatenate(
            special(block(head, s)) + ordinary(block(rest, 2 * s)) + ordinary(block(rest, 2 * s + 1)), axis=0
        )
        x = thirds(x)
        hid = product(x, weights[2 * s], NN, 3) + offset(s, 0)
        act = thirds(jnp.maximum(hid, 0.0))
        out = product(act, weights[2 * s + 1], NN, 3) + offset(s, 1)
        forward.append((x, hid, act, out))

    def backward(s, upstream):
        x, hid, act, out = forward[s]
        grad_out = jnp.where(jnp.abs(out) > SHRINK, upstream, 0.0)
        grad_out_halves = halves(grad_out)
        grad_hid = jnp.where(hid > 0.0, product(grad_out_halves, weights[2 * s + 1], NT), 0.0)
        grad_hid_halves = halves(grad_hid)
        grad_x = product(grad_hid_halves, weights[2 * s], NT)
        pairs = []
        for n, (left, right) in enumerate(((x, grad_hid_halves), (act, grad_out_halves))):
            full = product(left, right, TN)
            grads_ref[pl.ds((2 * n) * CH, CH), :] = full[:CH, :LANES] + full[LANES : LANES + CH, LANES:]
            grads_ref[pl.ds((2 * n + 1) * CH, CH), :] = full[:CH, LANES:] - full[LANES : LANES + CH, :LANES]
        offsets = []
        for value in (grad_hid, grad_out):
            total = jnp.sum(value, axis=0, keepdims=True)
            offsets += [total[:, :LANES], total[:, LANES:]]
        sums = []
        for c in (1, 2):
            one, two = grad_x[2 * c * H : (2 * c + 1) * H], grad_x[(2 * c + 1) * H : (2 * c + 2) * H]
            sums.append(
                jnp.concatenate([one[:, :LANES] + two[:, :LANES], one[:, LANES:] - two[:, LANES:]], axis=0)
            )
        lead = jnp.concatenate(
            [grad_x[:H, :LANES], grad_x[:H, LANES:], grad_x[H : 2 * H, :LANES], grad_x[H : 2 * H, LANES:]], axis=0
        )
        head_back = product(first_t, halves(lead), NN)
        rest_back = product(plain_t, halves(jnp.concatenate(sums, axis=1)), NN)
        return [head_back, block(rest_back, 0), block(rest_back, 1)], sums, offsets

    def emit(s, columns, offsets):
        values = {}
        for c in range(COLS):
            for of in range(2):
                for r in range(ROWS):
                    base = (of * ROWS + r) * N_SPACE
                    values[slot(of, c, r)] = columns[c][base : base + N_SPACE]
        share = 4 * CH // N_SPACE
        for j in range(share):
            values[N_FIELD + j] = grads_ref[pl.ds(j, N_SPACE, stride=share), :]
        for j in range(4):
            values[N_FIELD + share + j] = jnp.broadcast_to(offsets[j], (N_SPACE, LANES))

        def put(q, value):
            out_ref[pl.ds(s * N_SPACE * BLOCK + q, N_SPACE, stride=BLOCK), :] = value

        pack_rows(put, N_SPACE, values)

    fetch.wait()
    first_t = [first_t_ref[n] for n in range(2)]
    upstream = jnp.concatenate(
        special(adjoint_head) + ordinary(block(adjoint_rest, 0)) + ordinary(block(adjoint_rest, 1)), axis=0
    )
    columns_one, sums, offsets = backward(1, upstream)
    emit(1, columns_one, offsets)

    head_next = product(first, halves(adjoint_first + scale * columns_one[0]), NN)
    upstream = jnp.concatenate(
        special(head_next)
        + ordinary(block(adjoint_rest, 0) + 0.5 * sums[0])
        + ordinary(block(adjoint_rest, 1) + 0.5 * sums[1]),
        axis=0,
    )
    columns_zero, sums, offsets = backward(0, upstream)
    emit(0, [one + zero for one, zero in zip(columns_one, columns_zero)], offsets)


def total_kernel(got_ref, share_ref, offset_ref):
    total = got_ref[pl.ds(0, BLOCK), :]
    for d in range(1, N_DEST):
        total = total + got_ref[pl.ds(d * BLOCK, BLOCK), :]
    share = 4 * CH // N_SPACE
    lane = lane_index(16)
    late = jnp.zeros((16, LANES), F32)
    for third in range(3):
        moved = pltpu.roll(total[16 * third : 16 * third + 16], (32 * third - CH) % LANES, 1)
        late = jnp.where((lane >= 32 * third) & (lane < 32 * third + 32), moved, late)
    early = BLOCK - N_FIELD
    for p in range(N_SPACE):
        share_ref[pl.ds(p * share, early), :] = total[N_FIELD:BLOCK]
        share_ref[pl.ds(p * share + early, share - early), :] = late[: share - early]
    offset_ref[...] = late[share - early : 16]


def after_kernel(got_ref, g_ref, pair_ref, out_ref):
    for j in range(ROWS // 2):
        rows = []
        for rr in range(2):
            for of in range(2):
                for c in range(COLS):
                    rows.append(got_ref[pl.ds(slot(of, c, 2 * j + rr), N_DEST, stride=BLOCK), :])
        spectrum = halves(jnp.concatenate(rows, axis=0))
        back = product(spectrum, [pair_ref[n] for n in range(2)], TN)
        lanes = pl.ds(2 * W * j, 2 * W)
        out_ref[:, lanes] = g_ref[:, lanes] + back[:CH]


def vmem(count):
    return [pl.BlockSpec(memory_space=pltpu.VMEM)] * count


def smem():
    return [pl.BlockSpec(memory_space=pltpu.SMEM)]


PARAMS = pltpu.CompilerParams(vmem_limit_bytes=VMEM_LIMIT)


def shards(acts, cotangent, w_in, w_out, b_in, b_out):
    segment = lax.axis_index("segment")
    space = lax.axis_index("space")
    everyone = ("segment", "space")
    block_input, given = acts[0, 0], cotangent[0]

    plain, heads = height_tables()
    table_parts = split_table(width_table().reshape(2, COLS * N_DEST, W), 3)
    pair_parts = split_table(row_pair_table(), 2)
    plain_parts = split_table(plain, 3)
    plain_t_parts = split_table(plain.T, 2)
    head_parts = split_table(heads, 3)
    head_t_parts = split_table(heads.transpose(0, 2, 1), 2).swapaxes(0, 1)

    swap = [(0, 1), (1, 0)]
    own_w = [w_in[0, :, 0], w_out[0, :, 0]]
    other_w = [lax.ppermute(w, "segment", swap) for w in own_w]

    given_arrays = (block_input, given, b_in[0], b_out[0], table_parts)
    sent = pl.pallas_call(
        ahead_kernel,
        out_shape=jax.ShapeDtypeStruct((N_DEST * BLOCK, LANES), F32),
        in_specs=smem() + [pl.BlockSpec(memory_space=pl.ANY)] * len(given_arrays),
        out_specs=pl.BlockSpec(memory_space=pltpu.VMEM),
        scratch_shapes=[pltpu.VMEM(a.shape, a.dtype) for a in given_arrays]
        + [pltpu.SemaphoreType.DMA((len(given_arrays),))],
        compiler_params=pltpu.CompilerParams(vmem_limit_bytes=AHEAD_VMEM),
        name="ahead",
    )(segment.astype(jnp.int32).reshape(1), *given_arrays)
    sent, other_w = lax.optimization_barrier((sent, other_w))
    got = lax.all_to_all(sent.reshape(N_DEST, BLOCK, LANES), everyone, 0, 0, tiled=True)

    own_w, other_w = jnp.concatenate(own_w), jnp.concatenate(other_w)
    is_zero = segment == 0
    all_w = jnp.concatenate([jnp.where(is_zero, own_w, other_w), jnp.where(is_zero, other_w, own_w)])
    all_w = jnp.pad(all_w, ((0, 0), (0, LANES - CH), (0, LANES - CH))).reshape(4, 2, LANES, LANES)
    w0, w1 = all_w[:, 0], all_w[:, 1]
    full_w = jnp.concatenate(
        [jnp.concatenate([w0, w1], axis=2), jnp.concatenate([-w1, w0], axis=2)], axis=1
    )

    flag = ((segment == 0) & (space == 0)).astype(jnp.int32).reshape(1)
    sent = pl.pallas_call(
        middle_kernel,
        out_shape=jax.ShapeDtypeStruct((N_DEST * BLOCK, LANES), F32),
        in_specs=smem() + vmem(5) + [pl.BlockSpec(memory_space=pl.ANY)],
        out_specs=pl.BlockSpec(memory_space=pltpu.VMEM),
        scratch_shapes=[
            pltpu.VMEM((4 * CH, LANES), F32),
            pltpu.VMEM(head_t_parts.shape[1:], BF16),
            pltpu.SemaphoreType.DMA,
        ],
        compiler_params=PARAMS,
        name="middle",
    )(flag, got.reshape(N_DEST * BLOCK, LANES), full_w, plain_parts, plain_t_parts, head_parts, head_t_parts)
    got = lax.all_to_all(sent.reshape(N_DEST, BLOCK, LANES), everyone, 0, 0, tiled=True)
    got = got.reshape(N_DEST * BLOCK, LANES)

    share = 4 * CH // N_SPACE
    mine, offsets = pl.pallas_call(
        total_kernel,
        out_shape=(
            jax.ShapeDtypeStruct((N_SPACE * share, LANES), F32),
            jax.ShapeDtypeStruct((4, LANES), F32),
        ),
        in_specs=vmem(1),
        out_specs=tuple(vmem(2)),
        compiler_params=PARAMS,
        name="total",
    )(got)
    whole = lax.all_to_all(mine.reshape(N_SPACE, share, LANES), "space", 0, 0, tiled=True)

    adjoint = pl.pallas_call(
        after_kernel,
        out_shape=jax.ShapeDtypeStruct((CH, ROWS * W), F32),
        in_specs=vmem(3),
        out_specs=pl.BlockSpec(memory_space=pltpu.VMEM),
        compiler_params=PARAMS,
        name="after",
    )(got, given, pair_parts)

    whole = whole.reshape(4, CH, LANES)[:, :, :CH]
    offsets = offsets[:, :CH]
    return (
        adjoint[None, None],
        whole[:2].reshape(w_in.shape),
        whole[2:].reshape(w_out.shape),
        offsets[:2].reshape(b_in.shape),
        offsets[2:].reshape(b_out.shape),
    )


def solution(mesh):
    placed = (
        P("segment", None, "chan", "space"),
        P(None, "chan", "space"),
        P("segment", None, "chan", None, None),
        P("segment", None, "chan", None, None),
        P("segment", None, "chan"),
        P("segment", None, "chan"),
    )
    return jax.shard_map(
        shards,
        mesh=mesh,
        in_specs=placed,
        out_specs=(
            P("segment", None, "chan", "space"),
            P("segment", None, "chan", None, None),
            P("segment", None, "chan", None, None),
            P("segment", None, "chan"),
            P("segment", None, "chan"),
        ),
        check_vma=False,
    )
```

```python
import math

import jax
import jax.numpy as jnp
import ml_dtypes
import numpy as np
from jax import lax
from jax.experimental import pallas as pl
from jax.experimental.pallas import tpu as pltpu
from jax.sharding import PartitionSpec as P

H = 96
W = 192
CH = 96
LANES = 128
N_SPACE = 16
N_SEG = 2
N_X = 4
N_DEST = N_SPACE * N_SEG
ROWS = H // N_SPACE
COLS = W // 2 // N_DEST
BLOCK = 48
SHRINK = 0.3
BF16 = jnp.bfloat16
F32 = jnp.float32
VMEM_LIMIT = 24 * 1024 * 1024
AHEAD_VMEM = 56 * 1024 * 1024


def split_table(table, count):
    parts = []
    for _ in range(count):
        parts.append(table.astype(np.float32).astype(ml_dtypes.bfloat16))
        table = table - parts[-1].astype(np.float64)
    return np.stack(parts)


def dft(length):
    index = np.arange(length)
    phase = 2.0 * math.pi * (np.outer(index, index) % length) / length
    return np.cos(phase) / math.sqrt(length), np.sin(phase) / math.sqrt(length)


def width_table():
    cos_w, sin_w = dft(W)
    half = W // 2
    real, imag = cos_w[:half].copy(), -sin_w[:half].copy()
    imag[0] = cos_w[half]
    both = np.stack([real, imag])
    return both.reshape(2, N_DEST, COLS, W).transpose(0, 2, 1, 3)


def height_table():
    cos_h, sin_h = dft(H)
    order = np.array([ROWS * p + r for r in range(ROWS) for p in range(N_SPACE)])
    cos_h, sin_h = cos_h[np.ix_(order, order)], sin_h[np.ix_(order, order)]
    return np.block([[cos_h, sin_h], [-sin_h, cos_h]])


def row_pair_table():
    flat = width_table().reshape(2 * COLS * N_DEST, W)
    zero = np.zeros_like(flat)
    return np.block([[flat, zero], [zero, flat]])


def cut(value, count):
    parts = []
    for n in range(count):
        parts.append(value.astype(BF16))
        if n < count - 1:
            value = value - parts[-1].astype(F32)
    return parts


def halves(value):
    return cut(value, 2)


def thirds(value):
    return cut(value, 3)


def product(a, b, contract, parts=2):
    dims = (contract, ((), ()))
    total = None
    for order in reversed(range(parts)):
        for n in range(order + 1):
            one = lax.dot_general(a[n], b[order - n], dims, preferred_element_type=F32)
            total = one if total is None else total + one
    return total


NN = ((1,), (0,))
NT = ((1,), (1,))
TN = ((0,), (0,))


def lane_index(rows):
    return lax.broadcasted_iota(jnp.int32, (rows, LANES), 1)


def slot(part, c, r):
    return (part * COLS + c) * ROWS + r


N_FIELD = 2 * COLS * ROWS
OFFSET_ROW = N_FIELD + COLS * ROWS


def pack_rows(put, count, values):
    lane = lane_index(count)
    for q in range(BLOCK):
        third, extra = divmod(q, 16)
        value = values.get(q)
        packed = values.get(BLOCK + extra)
        if value is None:
            value = jnp.zeros((count, LANES), F32)
        if packed is not None:
            value = jnp.where(lane < CH, value, pltpu.roll(packed, CH - 32 * third, 1))
        put(q, value)


def unpack_row(get, count, q):
    if q < BLOCK:
        return get(q)
    lane = lane_index(count)
    extra = q - BLOCK
    value = jnp.zeros((count, LANES), F32)
    for third in range(3):
        moved = pltpu.roll(get(extra + 16 * third), (32 * third - CH) % LANES, 1)
        value = jnp.where((lane >= 32 * third) & (lane < 32 * third + 32), moved, value)
    return value


def ahead_kernel(
    seg_ref, x_hbm, g_hbm, b_in_hbm, b_out_hbm, table_hbm, out_ref, x_ref, g_ref, b_in_ref, b_out_ref, table_ref, sems
):
    segment = seg_ref[0]
    pairs = [
        (table_hbm, table_ref),
        (x_hbm, x_ref),
        (g_hbm, g_ref),
        (b_in_hbm, b_in_ref),
        (b_out_hbm, b_out_ref),
    ]
    copies = [pltpu.make_async_copy(src, dst, sems.at[n]) for n, (src, dst) in enumerate(pairs)]
    for copy in copies:
        copy.start()
    pad = jnp.zeros((LANES - CH, W), F32)
    values = {}

    def two_rows(ref, r):
        return jnp.concatenate([ref[:, pl.ds(W * r, W)], pad, ref[:, pl.ds(W * (r + 1), W)], pad], axis=0)

    copies[0].wait()
    table = [table_ref[n].reshape(2 * COLS * N_DEST, W) for n in range(3)]
    part = [table_ref[n, segment] for n in range(2)]
    copies[1].wait()
    for r in range(0, ROWS, 2):
        field = product(table, thirds(two_rows(x_ref, r)), NT, 3)
        for rr in range(2):
            for of in range(2):
                for c in range(COLS):
                    base = (of * COLS + c) * N_DEST
                    values[slot(of, c, r + rr)] = field[base : base + N_DEST, LANES * rr : LANES * (rr + 1)]
    copies[2].wait()
    for r in range(0, ROWS, 2):
        adjoint = product(part, halves(two_rows(g_ref, r)), NT)
        for rr in range(2):
            for c in range(COLS):
                base = c * N_DEST
                values[N_FIELD + c * ROWS + r + rr] = adjoint[base : base + N_DEST, LANES * rr : LANES * (rr + 1)]
    copies[3].wait()
    copies[4].wait()
    fill = jnp.zeros((1, LANES - CH), F32)
    for n, ref in enumerate((b_in_ref, b_out_ref)):
        for of in range(2):
            one = jnp.concatenate([ref[of : of + 1, :], fill], axis=1)
            values[OFFSET_ROW + 2 * n + of] = jnp.broadcast_to(one, (N_DEST, LANES))

    def put(q, value):
        out_ref[pl.ds(q, N_DEST, stride=BLOCK), :] = value

    pack_rows(put, N_DEST, values)


def middle_kernel(flag_ref, got_ref, w_ref, table_ref, out_ref, grads_ref):
    is_special = flag_ref[0] == 1
    table = [table_ref[n] for n in range(3)]
    scale = jnp.where(is_special, 1.0, 0.5).astype(F32)

    def row(source, q):
        def get(at):
            return got_ref[pl.ds(source * N_SPACE * BLOCK + at, N_SPACE, stride=BLOCK), :]

        return unpack_row(get, N_SPACE, q)

    def field_column(s, c):
        return jnp.concatenate([row(s, slot(of, c, r)) for of in range(2) for r in range(ROWS)], axis=0)

    def adjoint_column(c):
        return jnp.concatenate([row(of, N_FIELD + c * ROWS + r) for of in range(2) for r in range(ROWS)], axis=0)

    nothing = jnp.zeros((H, LANES), F32)

    def block(value, n):
        return value[:, LANES * n : LANES * (n + 1)]

    def spread(first):
        one = jnp.concatenate([first[:H], jnp.where(is_special, nothing, first[H:])], axis=0)
        return [one, jnp.concatenate([first[H:], nothing], axis=0)]

    def ordinary(column):
        r, i = column[:H], column[H:]
        return [jnp.concatenate([r, i], axis=1), jnp.concatenate([r, -i], axis=1)]

    def leading(one, two):
        mirror = jnp.where(is_special, two, jnp.concatenate([one[:H], -one[H:]], axis=0))
        return [jnp.concatenate([v[:H], v[H:]], axis=1) for v in (one, mirror)]

    def transform(columns, parts):
        return product(table, cut(jnp.concatenate(columns, axis=1), parts), NN, parts)

    adjoint_first = adjoint_column(0)
    fields = transform(
        [v for s in range(2) for v in spread(field_column(s, 0)) + [field_column(s, 1), field_column(s, 2)]], 3
    )
    adjoints = transform(spread(adjoint_first) + [adjoint_column(1), adjoint_column(2)], 2)

    weights = [thirds(w_ref[n]) for n in range(4)]

    def offset(s, n):
        def get(at):
            return got_ref[pl.ds(s * N_SPACE * BLOCK + at, 1), :]

        return jnp.concatenate([unpack_row(get, 1, OFFSET_ROW + 2 * n + of) for of in range(2)], axis=1)

    forward = []
    for s in range(2):
        parts = [block(fields, 4 * s + n) for n in range(4)]
        x = jnp.concatenate(leading(parts[0], parts[1]) + ordinary(parts[2]) + ordinary(parts[3]), axis=0)
        x = thirds(x)
        hid = product(x, weights[2 * s], NN, 3) + offset(s, 0)
        act = thirds(jnp.maximum(hid, 0.0))
        out = product(act, weights[2 * s + 1], NN, 3) + offset(s, 1)
        forward.append((x, hid, act, out))

    def backward(s, upstream):
        x, hid, act, out = forward[s]
        grad_out = jnp.where(jnp.abs(out) > SHRINK, upstream, 0.0)
        grad_out_halves = halves(grad_out)
        grad_hid = jnp.where(hid > 0.0, product(grad_out_halves, weights[2 * s + 1], NT), 0.0)
        grad_hid_halves = halves(grad_hid)
        grad_x = product(grad_hid_halves, weights[2 * s], NT)
        pairs = []
        for n, (left, right) in enumerate(((x, grad_hid_halves), (act, grad_out_halves))):
            full = product(left, right, TN)
            grads_ref[pl.ds((2 * n) * CH, CH), :] = full[:CH, :LANES] + full[LANES : LANES + CH, LANES:]
            grads_ref[pl.ds((2 * n + 1) * CH, CH), :] = full[:CH, LANES:] - full[LANES : LANES + CH, :LANES]
        offsets = []
        for value in (grad_hid, grad_out):
            total = jnp.sum(value, axis=0, keepdims=True)
            offsets += [total[:, :LANES], total[:, LANES:]]
        sums = []
        for c in range(COLS):
            one, two = grad_x[2 * c * H : (2 * c + 1) * H], grad_x[(2 * c + 1) * H : (2 * c + 2) * H]
            sums.append((one[:, :LANES] + two[:, :LANES], one[:, LANES:] - two[:, LANES:]))
        one = jnp.concatenate(
            [
                jnp.where(is_special, grad_x[:H, :LANES], sums[0][0]),
                -jnp.where(is_special, grad_x[:H, LANES:], sums[0][1]),
            ],
            axis=0,
        )
        two = jnp.concatenate([grad_x[H : 2 * H, :LANES], -grad_x[H : 2 * H, LANES:]], axis=0)
        back = transform([one, two] + [jnp.concatenate([r, -i], axis=0) for r, i in sums[1:]], 2)
        columns = []
        for n in (0, 2, 3):
            low = -block(back, n)[H:]
            if n == 0:
                low = jnp.where(is_special, block(back, 1)[:H], low)
            columns.append(jnp.concatenate([block(back, n)[:H], low], axis=0))
        return columns, [jnp.concatenate(pair, axis=0) for pair in sums[1:]], offsets

    def emit(s, columns, offsets):
        values = {}
        for c in range(COLS):
            for of in range(2):
                for r in range(ROWS):
                    base = (of * ROWS + r) * N_SPACE
                    values[slot(of, c, r)] = columns[c][base : base + N_SPACE]
        share = 4 * CH // N_SPACE
        for j in range(share):
            values[N_FIELD + j] = grads_ref[pl.ds(j, N_SPACE, stride=share), :]
        for j in range(4):
            values[N_FIELD + share + j] = jnp.broadcast_to(offsets[j], (N_SPACE, LANES))

        def put(q, value):
            out_ref[pl.ds(s * N_SPACE * BLOCK + q, N_SPACE, stride=BLOCK), :] = value

        pack_rows(put, N_SPACE, values)

    parts = [block(adjoints, n) for n in range(4)]
    upstream = jnp.concatenate(leading(parts[0], parts[1]) + ordinary(parts[2]) + ordinary(parts[3]), axis=0)
    columns_one, sums, offsets = backward(1, upstream)
    emit(1, columns_one, offsets)

    lead = transform(spread(adjoint_first + scale * columns_one[0]), 2)
    upstream = jnp.concatenate(
        leading(block(lead, 0), block(lead, 1))
        + ordinary(parts[2] + 0.5 * sums[0])
        + ordinary(parts[3] + 0.5 * sums[1]),
        axis=0,
    )
    columns_zero, sums, offsets = backward(0, upstream)
    emit(0, [one + zero for one, zero in zip(columns_one, columns_zero)], offsets)


def total_kernel(got_ref, share_ref, offset_ref):
    total = got_ref[pl.ds(0, BLOCK), :]
    for d in range(1, N_DEST):
        total = total + got_ref[pl.ds(d * BLOCK, BLOCK), :]
    share = 4 * CH // N_SPACE
    lane = lane_index(16)
    late = jnp.zeros((16, LANES), F32)
    for third in range(3):
        moved = pltpu.roll(total[16 * third : 16 * third + 16], (32 * third - CH) % LANES, 1)
        late = jnp.where((lane >= 32 * third) & (lane < 32 * third + 32), moved, late)
    early = BLOCK - N_FIELD
    for p in range(N_SPACE):
        share_ref[pl.ds(p * share, early), :] = total[N_FIELD:BLOCK]
        share_ref[pl.ds(p * share + early, share - early), :] = late[: share - early]
    offset_ref[...] = late[share - early : 16]


def after_kernel(got_ref, g_ref, pair_ref, out_ref):
    for j in range(ROWS // 2):
        rows = []
        for rr in range(2):
            for of in range(2):
                for c in range(COLS):
                    rows.append(got_ref[pl.ds(slot(of, c, 2 * j + rr), N_DEST, stride=BLOCK), :])
        spectrum = halves(jnp.concatenate(rows, axis=0))
        back = product(spectrum, [pair_ref[n] for n in range(2)], TN)
        lanes = pl.ds(2 * W * j, 2 * W)
        out_ref[:, lanes] = g_ref[:, lanes] + back[:CH]


def vmem(count):
    return [pl.BlockSpec(memory_space=pltpu.VMEM)] * count


def smem():
    return [pl.BlockSpec(memory_space=pltpu.SMEM)]


PARAMS = pltpu.CompilerParams(vmem_limit_bytes=VMEM_LIMIT)


def shards(acts, cotangent, w_in, w_out, b_in, b_out):
    segment = lax.axis_index("segment")
    space = lax.axis_index("space")
    everyone = ("segment", "space")
    block_input, given = acts[0, 0], cotangent[0]

    table_parts = split_table(width_table().reshape(2, COLS * N_DEST, W), 3)
    pair_parts = split_table(row_pair_table(), 2)
    height_parts = split_table(height_table(), 3)

    depth = N_DEST // N_X
    swap = [(z * N_X + x, (depth - 1 - z) * N_X + x) for z in range(depth) for x in range(N_X)]
    own_w = [w_in[0, :, 0], w_out[0, :, 0]]
    other_w = [lax.ppermute(w, everyone, swap) for w in own_w]

    given_arrays = (block_input, given, b_in[0], b_out[0], table_parts)
    sent = pl.pallas_call(
        ahead_kernel,
        out_shape=jax.ShapeDtypeStruct((N_DEST * BLOCK, LANES), F32),
        in_specs=smem() + [pl.BlockSpec(memory_space=pl.ANY)] * len(given_arrays),
        out_specs=pl.BlockSpec(memory_space=pltpu.VMEM),
        scratch_shapes=[pltpu.VMEM(a.shape, a.dtype) for a in given_arrays]
        + [pltpu.SemaphoreType.DMA((len(given_arrays),))],
        compiler_params=pltpu.CompilerParams(vmem_limit_bytes=AHEAD_VMEM),
        name="ahead",
    )(segment.astype(jnp.int32).reshape(1), *given_arrays)
    sent, other_w = lax.optimization_barrier((sent, other_w))
    got = lax.all_to_all(sent.reshape(N_DEST, BLOCK, LANES), everyone, 0, 0, tiled=True)

    own_w, other_w = jnp.concatenate(own_w), jnp.concatenate(other_w)
    is_zero = segment == 0
    all_w = jnp.concatenate([jnp.where(is_zero, own_w, other_w), jnp.where(is_zero, other_w, own_w)])
    all_w = jnp.pad(all_w, ((0, 0), (0, LANES - CH), (0, LANES - CH))).reshape(4, 2, LANES, LANES)
    w0, w1 = all_w[:, 0], all_w[:, 1]
    full_w = jnp.concatenate(
        [jnp.concatenate([w0, w1], axis=2), jnp.concatenate([-w1, w0], axis=2)], axis=1
    )

    flag = ((segment == 0) & (space == 0)).astype(jnp.int32).reshape(1)
    sent = pl.pallas_call(
        middle_kernel,
        out_shape=jax.ShapeDtypeStruct((N_DEST * BLOCK, LANES), F32),
        in_specs=smem() + vmem(3),
        out_specs=pl.BlockSpec(memory_space=pltpu.VMEM),
        scratch_shapes=[pltpu.VMEM((4 * CH, LANES), F32)],
        compiler_params=PARAMS,
        name="middle",
    )(flag, got.reshape(N_DEST * BLOCK, LANES), full_w, height_parts)
    got = lax.all_to_all(sent.reshape(N_DEST, BLOCK, LANES), everyone, 0, 0, tiled=True)
    got = got.reshape(N_DEST * BLOCK, LANES)

    share = 4 * CH // N_SPACE
    mine, offsets = pl.pallas_call(
        total_kernel,
        out_shape=(
            jax.ShapeDtypeStruct((N_SPACE * share, LANES), F32),
            jax.ShapeDtypeStruct((4, LANES), F32),
        ),
        in_specs=vmem(1),
        out_specs=tuple(vmem(2)),
        compiler_params=PARAMS,
        name="total",
    )(got)
    whole = lax.all_to_all(mine.reshape(N_SPACE, share, LANES), "space", 0, 0, tiled=True)

    adjoint = pl.pallas_call(
        after_kernel,
        out_shape=jax.ShapeDtypeStruct((CH, ROWS * W), F32),
        in_specs=vmem(3),
        out_specs=pl.BlockSpec(memory_space=pltpu.VMEM),
        compiler_params=PARAMS,
        name="after",
    )(got, given, pair_parts)

    whole = whole.reshape(4, CH, LANES)[:, :, :CH]
    offsets = offsets[:, :CH]
    return (
        adjoint[None, None],
        whole[:2].reshape(w_in.shape),
        whole[2:].reshape(w_out.shape),
        offsets[:2].reshape(b_in.shape),
        offsets[2:].reshape(b_out.shape),
    )


def solution(mesh):
    placed = (
        P("segment", None, "chan", "space"),
        P(None, "chan", "space"),
        P("segment", None, "chan", None, None),
        P("segment", None, "chan", None, None),
        P("segment", None, "chan"),
        P("segment", None, "chan"),
    )
    return jax.shard_map(
        shards,
        mesh=mesh,
        in_specs=placed,
        out_specs=(
            P("segment", None, "chan", "space"),
            P("segment", None, "chan", None, None),
            P("segment", None, "chan", None, None),
            P("segment", None, "chan"),
            P("segment", None, "chan"),
        ),
        check_vma=False,
    )
```

```python
import math

import jax
import jax.numpy as jnp
import ml_dtypes
import numpy as np
from jax import lax
from jax.experimental import pallas as pl
from jax.experimental.pallas import tpu as pltpu
from jax.sharding import PartitionSpec as P

H = 96
W = 192
CH = 96
LANES = 128
N_SPACE = 16
N_SEG = 2
N_DEST = N_SPACE * N_SEG
ROWS = H // N_SPACE
COLS = W // 2 // N_DEST
EXTRA = 16
BLOCK_IN = 56
BLOCK_OUT = 48
SHRINK = 0.3
BF16 = jnp.bfloat16
F32 = jnp.float32
VMEM_LIMIT = 24 * 1024 * 1024
AHEAD_VMEM = 56 * 1024 * 1024


def split_table(table, count):
    parts = []
    for _ in range(count):
        parts.append(table.astype(np.float32).astype(ml_dtypes.bfloat16))
        table = table - parts[-1].astype(np.float64)
    return np.stack(parts)


def dft(length):
    index = np.arange(length)
    phase = 2.0 * math.pi * (np.outer(index, index) % length) / length
    return np.cos(phase) / math.sqrt(length), np.sin(phase) / math.sqrt(length)


def width_table():
    cos_w, sin_w = dft(W)
    half = W // 2
    real, imag = cos_w[:half].copy(), -sin_w[:half].copy()
    imag[0] = cos_w[half]
    both = np.stack([real, imag])
    return both.reshape(2, N_DEST, COLS, W).transpose(0, 2, 1, 3)


def height_table():
    cos_h, sin_h = dft(H)
    order = np.array([ROWS * p + r for r in range(ROWS) for p in range(N_SPACE)])
    cos_h, sin_h = cos_h[np.ix_(order, order)], sin_h[np.ix_(order, order)]
    return np.block([[cos_h, sin_h], [-sin_h, cos_h]])


def row_pair_table():
    flat = width_table().reshape(2 * COLS * N_DEST, W)
    zero = np.zeros_like(flat)
    return np.block([[flat, zero], [zero, flat]])


def cut(value, count):
    parts = []
    for n in range(count):
        parts.append(value.astype(BF16))
        if n < count - 1:
            value = value - parts[-1].astype(F32)
    return parts


def halves(value):
    return cut(value, 2)


def thirds(value):
    return cut(value, 3)


def product(a, b, contract, parts=2):
    dims = (contract, ((), ()))
    total = None
    for order in reversed(range(parts)):
        for n in range(order + 1):
            one = lax.dot_general(a[n], b[order - n], dims, preferred_element_type=F32)
            total = one if total is None else total + one
    return total


NN = ((1,), (0,))
NT = ((1,), (1,))
TN = ((0,), (0,))


def lane_index(rows):
    return lax.broadcasted_iota(jnp.int32, (rows, LANES), 1)


def slot(part, c, r):
    return (part * COLS + c) * ROWS + r


N_FIELD = 2 * COLS * ROWS
WEIGHT_ROW = N_FIELD + 4
SHARE = 4 * CH // N_SPACE


def pack_rows(put, count, values, block):
    lane = lane_index(count)
    for q in range(block):
        value = values.get(q)
        if value is None:
            value = jnp.zeros((count, LANES), F32)
        third, extra = divmod(q, EXTRA)
        packed = values.get(block + extra)
        if packed is not None and third < 3:
            value = jnp.where(lane < CH, value, pltpu.roll(packed, CH - 32 * third, 1))
        put(q, value)


def join_thirds(thirds_of):
    lane = lane_index(thirds_of[0].shape[0])
    value = jnp.zeros(thirds_of[0].shape, F32)
    for third, part in enumerate(thirds_of):
        moved = pltpu.roll(part, (32 * third - CH) % LANES, 1)
        value = jnp.where((lane >= 32 * third) & (lane < 32 * third + 32), moved, value)
    return value


def unpack_row(get, q, block):
    if q < block:
        return get(q)
    return join_thirds([get(q - block + EXTRA * third) for third in range(3)])


def ahead_kernel(
    place_ref, x_hbm, g_hbm, b_in_hbm, b_out_hbm, w_in_hbm, w_out_hbm, table_hbm,
    out_ref, x_ref, g_ref, b_in_ref, b_out_ref, w_ref, table_ref, sems,
):
    segment, space = place_ref[0], place_ref[1]
    pairs = [(table_hbm, table_ref)]
    for src, dst in ((x_hbm, x_ref), (g_hbm, g_ref)):
        for j in range(ROWS // 2):
            lanes = pl.ds(2 * W * j, 2 * W)
            pairs.append((src.at[:, lanes], dst.at[:, lanes]))
    pairs += [(b_in_hbm, b_in_ref), (b_out_hbm, b_out_ref), (w_in_hbm, w_ref.at[0:2]), (w_out_hbm, w_ref.at[2:4])]
    copies = [pltpu.make_async_copy(src, dst, sems.at[n]) for n, (src, dst) in enumerate(pairs)]
    for copy in copies:
        copy.start()
    pad = jnp.zeros((LANES - CH, W), F32)
    fields = [{} for _ in range(N_SEG)]
    adjoints = {}

    def two_rows(ref, r):
        return jnp.concatenate([ref[:, pl.ds(W * r, W)], pad, ref[:, pl.ds(W * (r + 1), W)], pad], axis=0)

    def cut_out(value, base, rr):
        return value[base : base + N_SPACE, LANES * rr : LANES * (rr + 1)]

    copies[0].wait()
    table = [table_ref[n].reshape(N_SEG * 2 * COLS * N_SPACE, W) for n in range(3)]
    part = [table_ref[n, segment] for n in range(2)]
    for r in range(0, ROWS, 2):
        copies[1 + r // 2].wait()
        field = product(table, thirds(two_rows(x_ref, r)), NT, 3)
        for rr in range(2):
            for s in range(N_SEG):
                for of in range(2):
                    for c in range(COLS):
                        fields[s][slot(of, c, r + rr)] = cut_out(field, ((s * 2 + of) * COLS + c) * N_SPACE, rr)
    for r in range(0, ROWS, 2):
        copies[1 + ROWS // 2 + r // 2].wait()
        adjoint = product(part, halves(two_rows(g_ref, r)), NT)
        for rr in range(2):
            for of in range(2):
                for c in range(COLS):
                    adjoints[N_FIELD + slot(of, c, r + rr)] = cut_out(adjoint, (of * COLS + c) * N_SPACE, rr)
    for copy in copies[1 + ROWS :]:
        copy.wait()
    others = {}

    def to_all(row):
        return jnp.broadcast_to(row, (N_SPACE, LANES))

    fill = jnp.zeros((1, LANES - CH), F32)
    for n, ref in enumerate((b_in_ref, b_out_ref)):
        for of in range(2):
            others[N_FIELD + 2 * n + of] = to_all(jnp.concatenate([ref[of : of + 1, :], fill], axis=1))
    start = pl.multiple_of(lax.rem(space, 4) * SHARE, 8)
    weights = w_ref[space // 4, pl.ds(start, SHARE), :]
    weights = jnp.concatenate([weights, jnp.zeros((SHARE, LANES - CH), F32)], axis=1)
    for j in range(SHARE):
        others[WEIGHT_ROW + j] = to_all(weights[j : j + 1])
    nothing = jnp.zeros((N_SPACE, LANES), F32)

    for s in range(N_SEG):
        values = dict(fields[s])
        for q in range(N_FIELD, 2 * N_FIELD):
            values[q] = jnp.where(segment == s, adjoints[q], others.get(q, nothing))

        def put(q, value, s=s):
            out_ref[pl.ds(s * N_SPACE * BLOCK_IN + q, N_SPACE, stride=BLOCK_IN), :] = value

        pack_rows(put, N_SPACE, values, BLOCK_IN)


def middle_kernel(place_ref, got_ref, own_w_ref, own_b_ref, table_ref, out_ref, grads_ref, w_ref, b_ref):
    segment, space = place_ref[0], place_ref[1]
    is_special = (segment == 0) & (space == 0)
    table = [table_ref[n] for n in range(3)]
    scale = jnp.where(is_special, 1.0, 0.5).astype(F32)

    def row(source, q):
        def get(at):
            return got_ref[pl.ds(source * N_SPACE * BLOCK_IN + at, N_SPACE, stride=BLOCK_IN), :]

        return unpack_row(get, q, BLOCK_IN)

    def field_column(s, c):
        return jnp.concatenate([row(s, slot(of, c, r)) for of in range(2) for r in range(ROWS)], axis=0)

    def adjoint_column(c):
        return jnp.concatenate(
            [row(segment, N_FIELD + slot(of, c, r)) for of in range(2) for r in range(ROWS)], axis=0
        )

    other = 1 - segment
    w_ref[segment] = own_w_ref[...]
    b_ref[segment] = own_b_ref[...]
    for n in range(4):
        b_ref[other, n : n + 1, :] = row(other, N_FIELD + n)[:1]
        for a in range(4):
            base = pl.multiple_of((other * N_SPACE + 4 * n + a) * BLOCK_IN, 8)
            main = got_ref[pl.ds(base + WEIGHT_ROW, BLOCK_IN - WEIGHT_ROW), :]
            main = jnp.where(lane_index(BLOCK_IN - WEIGHT_ROW) < CH, main, 0.0)
            rest = join_thirds([got_ref[pl.ds(base + EXTRA * third, 8), :] for third in range(3)])
            w_ref[other, n, pl.ds(SHARE * a, BLOCK_IN - WEIGHT_ROW), :] = main
            w_ref[other, n, pl.ds(SHARE * a + BLOCK_IN - WEIGHT_ROW, 8), :] = rest

    nothing = jnp.zeros((H, LANES), F32)

    def block(value, n):
        return value[:, LANES * n : LANES * (n + 1)]

    def spread(first):
        one = jnp.concatenate([first[:H], jnp.where(is_special, nothing, first[H:])], axis=0)
        return [one, jnp.concatenate([first[H:], nothing], axis=0)]

    def ordinary(column):
        r, i = column[:H], column[H:]
        return [jnp.concatenate([r, i], axis=1), jnp.concatenate([r, -i], axis=1)]

    def leading(one, two):
        mirror = jnp.where(is_special, two, jnp.concatenate([one[:H], -one[H:]], axis=0))
        return [jnp.concatenate([v[:H], v[H:]], axis=1) for v in (one, mirror)]

    def transform(columns, parts):
        return product(table, cut(jnp.concatenate(columns, axis=1), parts), NN, parts)

    adjoint_first = adjoint_column(0)
    fields = transform(
        [v for s in range(2) for v in spread(field_column(s, 0)) + [field_column(s, 1), field_column(s, 2)]], 3
    )
    adjoints = transform(spread(adjoint_first) + [adjoint_column(1), adjoint_column(2)], 2)

    weights = []
    gap = jnp.zeros((LANES - CH, 2 * LANES), F32)
    for s in range(N_SEG):
        for n in range(2):
            real, imag = w_ref[s, 2 * n], w_ref[s, 2 * n + 1]
            top, bottom = jnp.concatenate([real, imag], axis=1), jnp.concatenate([-imag, real], axis=1)
            weights.append(thirds(jnp.concatenate([top, gap, bottom, gap], axis=0)))

    def offset(s, n):
        return jnp.concatenate([b_ref[s, 2 * n + of : 2 * n + of + 1, :] for of in range(2)], axis=1)

    forward = []
    for s in range(2):
        parts = [block(fields, 4 * s + n) for n in range(4)]
        x = jnp.concatenate(leading(parts[0], parts[1]) + ordinary(parts[2]) + ordinary(parts[3]), axis=0)
        x = thirds(x)
        hid = product(x, weights[2 * s], NN, 3) + offset(s, 0)
        act = thirds(jnp.maximum(hid, 0.0))
        out = product(act, weights[2 * s + 1], NN, 3) + offset(s, 1)
        forward.append((x, hid, act, out))

    def backward(s, upstream):
        x, hid, act, out = forward[s]
        grad_out = jnp.where(jnp.abs(out) > SHRINK, upstream, 0.0)
        grad_out_halves = halves(grad_out)
        grad_hid = jnp.where(hid > 0.0, product(grad_out_halves, weights[2 * s + 1], NT), 0.0)
        grad_hid_halves = halves(grad_hid)
        grad_x = product(grad_hid_halves, weights[2 * s], NT)
        pairs = []
        for n, (left, right) in enumerate(((x, grad_hid_halves), (act, grad_out_halves))):
            full = product(left, right, TN)
            grads_ref[pl.ds((2 * n) * CH, CH), :] = full[:CH, :LANES] + full[LANES : LANES + CH, LANES:]
            grads_ref[pl.ds((2 * n + 1) * CH, CH), :] = full[:CH, LANES:] - full[LANES : LANES + CH, :LANES]
        offsets = []
        for value in (grad_hid, grad_out):
            total = jnp.sum(value, axis=0, keepdims=True)
            offsets += [total[:, :LANES], total[:, LANES:]]
        sums = []
        for c in range(COLS):
            one, two = grad_x[2 * c * H : (2 * c + 1) * H], grad_x[(2 * c + 1) * H : (2 * c + 2) * H]
            sums.append((one[:, :LANES] + two[:, :LANES], one[:, LANES:] - two[:, LANES:]))
        one = jnp.concatenate(
            [
                jnp.where(is_special, grad_x[:H, :LANES], sums[0][0]),
                -jnp.where(is_special, grad_x[:H, LANES:], sums[0][1]),
            ],
            axis=0,
        )
        two = jnp.concatenate([grad_x[H : 2 * H, :LANES], -grad_x[H : 2 * H, LANES:]], axis=0)
        back = transform([one, two] + [jnp.concatenate([r, -i], axis=0) for r, i in sums[1:]], 2)
        columns = []
        for n in (0, 2, 3):
            low = -block(back, n)[H:]
            if n == 0:
                low = jnp.where(is_special, block(back, 1)[:H], low)
            columns.append(jnp.concatenate([block(back, n)[:H], low], axis=0))
        return columns, [jnp.concatenate(pair, axis=0) for pair in sums[1:]], offsets

    def emit(s, columns, offsets):
        values = {}
        for c in range(COLS):
            for of in range(2):
                for r in range(ROWS):
                    base = (of * ROWS + r) * N_SPACE
                    values[slot(of, c, r)] = columns[c][base : base + N_SPACE]
        for j in range(SHARE):
            values[N_FIELD + j] = grads_ref[pl.ds(j, N_SPACE, stride=SHARE), :]
        for j in range(4):
            values[N_FIELD + SHARE + j] = jnp.broadcast_to(offsets[j], (N_SPACE, LANES))

        def put(q, value):
            out_ref[pl.ds(s * N_SPACE * BLOCK_OUT + q, N_SPACE, stride=BLOCK_OUT), :] = value

        pack_rows(put, N_SPACE, values, BLOCK_OUT)

    parts = [block(adjoints, n) for n in range(4)]
    upstream = jnp.concatenate(leading(parts[0], parts[1]) + ordinary(parts[2]) + ordinary(parts[3]), axis=0)
    columns_one, sums, offsets = backward(1, upstream)
    emit(1, columns_one, offsets)

    lead = transform(spread(adjoint_first + scale * columns_one[0]), 2)
    upstream = jnp.concatenate(
        leading(block(lead, 0), block(lead, 1))
        + ordinary(parts[2] + 0.5 * sums[0])
        + ordinary(parts[3] + 0.5 * sums[1]),
        axis=0,
    )
    columns_zero, sums, offsets = backward(0, upstream)
    emit(0, [one + zero for one, zero in zip(columns_one, columns_zero)], offsets)


def total_kernel(got_ref, share_ref, offset_ref):
    total = got_ref[pl.ds(0, BLOCK_OUT), :]
    for d in range(1, N_DEST):
        total = total + got_ref[pl.ds(d * BLOCK_OUT, BLOCK_OUT), :]
    late = join_thirds([total[EXTRA * third : EXTRA * (third + 1)] for third in range(3)])
    early = BLOCK_OUT - N_FIELD
    for p in range(N_SPACE):
        share_ref[pl.ds(p * SHARE, early), :] = total[N_FIELD:BLOCK_OUT]
        share_ref[pl.ds(p * SHARE + early, SHARE - early), :] = late[: SHARE - early]
    offset_ref[...] = late[SHARE - early : EXTRA]


def after_kernel(got_ref, g_ref, pair_ref, out_ref):
    for j in range(ROWS // 2):
        rows = []
        for rr in range(2):
            for of in range(2):
                for c in range(COLS):
                    rows.append(got_ref[pl.ds(slot(of, c, 2 * j + rr), N_DEST, stride=BLOCK_OUT), :])
        spectrum = halves(jnp.concatenate(rows, axis=0))
        back = product(spectrum, [pair_ref[n] for n in range(2)], TN)
        lanes = pl.ds(2 * W * j, 2 * W)
        out_ref[:, lanes] = g_ref[:, lanes] + back[:CH]


def vmem(count):
    return [pl.BlockSpec(memory_space=pltpu.VMEM)] * count


def smem():
    return [pl.BlockSpec(memory_space=pltpu.SMEM)]


PARAMS = pltpu.CompilerParams(vmem_limit_bytes=VMEM_LIMIT)


def shards(acts, cotangent, w_in, w_out, b_in, b_out):
    segment = lax.axis_index("segment")
    space = lax.axis_index("space")
    everyone = ("segment", "space")
    block_input, given = acts[0, 0], cotangent[0]

    by_owner = width_table().reshape(2, COLS, N_SEG, N_SPACE, W).transpose(2, 0, 1, 3, 4)
    table_parts = split_table(by_owner.reshape(N_SEG, 2 * COLS * N_SPACE, W), 3)
    pair_parts = split_table(row_pair_table(), 2)
    height_parts = split_table(height_table(), 3)

    place = jnp.stack([segment, space]).astype(jnp.int32)
    given_arrays = (block_input, given, b_in[0], b_out[0], w_in[0, :, 0], w_out[0, :, 0], table_parts)
    copied = [(CH, ROWS * W), (CH, ROWS * W), (2, CH), (2, CH), (4, CH, CH)]
    sent = pl.pallas_call(
        ahead_kernel,
        out_shape=jax.ShapeDtypeStruct((N_DEST * BLOCK_IN, LANES), F32),
        in_specs=smem() + [pl.BlockSpec(memory_space=pl.ANY)] * len(given_arrays),
        out_specs=pl.BlockSpec(memory_space=pltpu.VMEM),
        scratch_shapes=[pltpu.VMEM(shape, F32) for shape in copied]
        + [pltpu.VMEM(table_parts.shape, BF16), pltpu.SemaphoreType.DMA((1 + ROWS + 4,))],
        compiler_params=pltpu.CompilerParams(vmem_limit_bytes=AHEAD_VMEM),
        name="ahead",
    )(place, *given_arrays)
    got = lax.all_to_all(sent.reshape(N_DEST, BLOCK_IN, LANES), everyone, 0, 0, tiled=True)

    own_w = jnp.concatenate([w_in[0, :, 0], w_out[0, :, 0]])
    own_w = jnp.pad(own_w, ((0, 0), (0, 0), (0, LANES - CH)))
    own_b = jnp.pad(jnp.concatenate([b_in[0], b_out[0]]), ((0, 4), (0, LANES - CH)))

    sent = pl.pallas_call(
        middle_kernel,
        out_shape=jax.ShapeDtypeStruct((N_DEST * BLOCK_OUT, LANES), F32),
        in_specs=smem() + vmem(4),
        out_specs=pl.BlockSpec(memory_space=pltpu.VMEM),
        scratch_shapes=[
            pltpu.VMEM((4 * CH, LANES), F32),
            pltpu.VMEM((N_SEG, 4, CH, LANES), F32),
            pltpu.VMEM((N_SEG, 8, LANES), F32),
        ],
        compiler_params=PARAMS,
        name="middle",
    )(place, got.reshape(N_DEST * BLOCK_IN, LANES), own_w, own_b, height_parts)
    got = lax.all_to_all(sent.reshape(N_DEST, BLOCK_OUT, LANES), everyone, 0, 0, tiled=True)
    got = got.reshape(N_DEST * BLOCK_OUT, LANES)

    mine, offsets = pl.pallas_call(
        total_kernel,
        out_shape=(
            jax.ShapeDtypeStruct((N_SPACE * SHARE, LANES), F32),
            jax.ShapeDtypeStruct((4, LANES), F32),
        ),
        in_specs=vmem(1),
        out_specs=tuple(vmem(2)),
        compiler_params=PARAMS,
        name="total",
    )(got)
    whole = lax.all_to_all(mine.reshape(N_SPACE, SHARE, LANES), "space", 0, 0, tiled=True)

    adjoint = pl.pallas_call(
        after_kernel,
        out_shape=jax.ShapeDtypeStruct((CH, ROWS * W), F32),
        in_specs=vmem(3),
        out_specs=pl.BlockSpec(memory_space=pltpu.VMEM),
        compiler_params=PARAMS,
        name="after",
    )(got, given, pair_parts)

    whole = whole.reshape(4, CH, LANES)[:, :, :CH]
    offsets = offsets[:, :CH]
    return (
        adjoint[None, None],
        whole[:2].reshape(w_in.shape),
        whole[2:].reshape(w_out.shape),
        offsets[:2].reshape(b_in.shape),
        offsets[2:].reshape(b_out.shape),
    )


def solution(mesh):
    placed = (
        P("segment", None, "chan", "space"),
        P(None, "chan", "space"),
        P("segment", None, "chan", None, None),
        P("segment", None, "chan", None, None),
        P("segment", None, "chan"),
        P("segment", None, "chan"),
    )
    return jax.shard_map(
        shards,
        mesh=mesh,
        in_specs=placed,
        out_specs=(
            P("segment", None, "chan", "space"),
            P("segment", None, "chan", None, None),
            P("segment", None, "chan", None, None),
            P("segment", None, "chan"),
            P("segment", None, "chan"),
        ),
        check_vma=False,
    )
```

```python
import math

import jax
import jax.numpy as jnp
import ml_dtypes
import numpy as np
from jax import lax
from jax.experimental import pallas as pl
from jax.experimental.pallas import tpu as pltpu
from jax.sharding import PartitionSpec as P

H = 96
W = 192
CH = 96
LANES = 128
N_SPACE = 16
N_SEG = 2
N_DEST = N_SPACE * N_SEG
ROWS = H // N_SPACE
COLS = W // 2 // N_DEST
BLOCK_IN, EXTRA_IN = 51, 17
BLOCK_OUT, EXTRA_OUT = 48, 16
SHRINK = 0.3
BF16 = jnp.bfloat16
F32 = jnp.float32
VMEM_LIMIT = 24 * 1024 * 1024
AHEAD_VMEM = 56 * 1024 * 1024


def split_table(table, count):
    parts = []
    for _ in range(count):
        parts.append(table.astype(np.float32).astype(ml_dtypes.bfloat16))
        table = table - parts[-1].astype(np.float64)
    return np.stack(parts)


def dft(length):
    index = np.arange(length)
    phase = 2.0 * math.pi * (np.outer(index, index) % length) / length
    return np.cos(phase) / math.sqrt(length), np.sin(phase) / math.sqrt(length)


def width_table():
    cos_w, sin_w = dft(W)
    half = W // 2
    real, imag = cos_w[:half].copy(), -sin_w[:half].copy()
    imag[0] = cos_w[half]
    both = np.stack([real, imag])
    return both.reshape(2, N_DEST, COLS, W).transpose(0, 2, 1, 3)


def height_table():
    cos_h, sin_h = dft(H)
    order = np.array([ROWS * p + r for r in range(ROWS) for p in range(N_SPACE)])
    cos_h, sin_h = cos_h[np.ix_(order, order)], sin_h[np.ix_(order, order)]
    return np.block([[cos_h, sin_h], [-sin_h, cos_h]])


def row_pair_table():
    flat = width_table().reshape(2 * COLS * N_DEST, W)
    zero = np.zeros_like(flat)
    return np.block([[flat, zero], [zero, flat]])


def cut(value, count):
    parts = []
    for n in range(count):
        parts.append(value.astype(BF16))
        if n < count - 1:
            value = value - parts[-1].astype(F32)
    return parts


def halves(value):
    return cut(value, 2)


def thirds(value):
    return cut(value, 3)


def product(a, b, contract, parts=2):
    dims = (contract, ((), ()))
    total = None
    for order in reversed(range(parts)):
        for n in range(order + 1):
            one = lax.dot_general(a[n], b[order - n], dims, preferred_element_type=F32)
            total = one if total is None else total + one
    return total


NN = ((1,), (0,))
NT = ((1,), (1,))
TN = ((0,), (0,))


def lane_index(rows):
    return lax.broadcasted_iota(jnp.int32, (rows, LANES), 1)


def slot(part, c, r):
    return (part * COLS + c) * ROWS + r


N_FIELD = 2 * COLS * ROWS
OWN = 32
OFFSET_ROW = 2 * N_FIELD - OWN
WEIGHT_ROW = OFFSET_ROW + 4
SHARE = 4 * CH // N_SPACE


def pack_rows(put, count, values, block, extras):
    lane = lane_index(count)
    for q in range(block):
        third, extra = divmod(q, extras)
        value = values[q]
        if third < 3:
            value = jnp.where(lane < CH, value, pltpu.roll(values[block + extra], CH - 32 * third, 1))
        put(q, value)


def join_thirds(thirds_of):
    lane = lane_index(thirds_of[0].shape[0])
    value = jnp.zeros(thirds_of[0].shape, F32)
    for third, part in enumerate(thirds_of):
        moved = pltpu.roll(part, (32 * third - CH) % LANES, 1)
        value = jnp.where((lane >= 32 * third) & (lane < 32 * third + 32), moved, value)
    return value


def unpack_row(get, q, block, extras):
    if q < block:
        return get(q)
    return join_thirds([get(q - block + extras * third) for third in range(3)])


def ahead_kernel(
    x_hbm, g_hbm, b_in_hbm, b_out_hbm, w_in_hbm, w_out_hbm, table_hbm,
    out_ref, x_ref, g_ref, b_in_ref, b_out_ref, w_ref, table_ref, sems,
):
    segment, space = lax.axis_index("segment"), lax.axis_index("space")
    pairs = [(table_hbm, table_ref)]
    for src, dst in ((x_hbm, x_ref), (g_hbm, g_ref)):
        for j in range(ROWS // 2):
            lanes = pl.ds(2 * W * j, 2 * W)
            pairs.append((src.at[:, lanes], dst.at[:, lanes]))
    pairs += [(b_in_hbm, b_in_ref), (b_out_hbm, b_out_ref), (w_in_hbm, w_ref.at[0:2]), (w_out_hbm, w_ref.at[2:4])]
    copies = [pltpu.make_async_copy(src, dst, sems.at[n]) for n, (src, dst) in enumerate(pairs)]
    for copy in copies:
        copy.start()
    pad = jnp.zeros((LANES - CH, W), F32)
    fields = [{} for _ in range(N_SEG)]
    adjoints = {}

    def two_rows(ref, r):
        return jnp.concatenate([ref[:, pl.ds(W * r, W)], pad, ref[:, pl.ds(W * (r + 1), W)], pad], axis=0)

    def cut_out(value, base, rr):
        return value[base : base + N_SPACE, LANES * rr : LANES * (rr + 1)]

    copies[0].wait()
    table = [table_ref[n].reshape(N_SEG * 2 * COLS * N_SPACE, W) for n in range(3)]
    last = (2 * COLS - 1) * N_SPACE
    part = [
        jnp.concatenate([table_ref[n, segment], table_ref[n, 1 - segment, last:, :]], axis=0) for n in range(2)
    ]
    others = {}
    for r in range(0, ROWS, 2):
        copies[1 + r // 2].wait()
        field = product(table, thirds(two_rows(x_ref, r)), NT, 3)
        for rr in range(2):
            for s in range(N_SEG):
                for of in range(2):
                    for c in range(COLS):
                        fields[s][slot(of, c, r + rr)] = cut_out(field, ((s * 2 + of) * COLS + c) * N_SPACE, rr)
    for r in range(0, ROWS, 2):
        copies[1 + ROWS // 2 + r // 2].wait()
        adjoint = product(part, halves(two_rows(g_ref, r)), NT)
        for rr in range(2):
            for of in range(2):
                for c in range(COLS):
                    at = slot(of, c, r + rr)
                    if at < OWN:
                        adjoints[N_FIELD + at] = cut_out(adjoint, (of * COLS + c) * N_SPACE, rr)
                    else:
                        others[N_FIELD + at - OWN] = cut_out(adjoint, last + N_SPACE, rr)
    for copy in copies[1 + ROWS :]:
        copy.wait()

    def to_all(row):
        return jnp.broadcast_to(row, (N_SPACE, LANES))

    fill = jnp.zeros((1, LANES - CH), F32)
    for n, ref in enumerate((b_in_ref, b_out_ref)):
        for of in range(2):
            others[OFFSET_ROW + 2 * n + of] = to_all(jnp.concatenate([ref[of : of + 1, :], fill], axis=1))
    start = pl.multiple_of(lax.rem(space, 4) * SHARE, 8)
    weights = w_ref[space // 4, pl.ds(start, SHARE), :]
    weights = jnp.concatenate([weights, jnp.zeros((SHARE, LANES - CH), F32)], axis=1)
    for j in range(SHARE):
        others[WEIGHT_ROW + j] = to_all(weights[j : j + 1])

    for s in range(N_SEG):
        values = dict(fields[s])
        for q in range(N_FIELD, N_FIELD + OWN):
            values[q] = jnp.where(segment == s, adjoints[q], others[q])

        def put(q, value, s=s):
            out_ref[pl.ds(s * N_SPACE * BLOCK_IN + q, N_SPACE, stride=BLOCK_IN), :] = value

        pack_rows(put, N_SPACE, values, BLOCK_IN, EXTRA_IN)


def middle_kernel(got_ref, own_w_ref, own_b_ref, table_ref, out_ref, grads_ref, w_ref, b_ref):
    segment, space = lax.axis_index("segment"), lax.axis_index("space")
    is_special = (segment == 0) & (space == 0)
    table = [table_ref[n] for n in range(3)]
    scale = jnp.where(is_special, 1.0, 0.5).astype(F32)

    def row(source, q):
        def get(at):
            return got_ref[pl.ds(source * N_SPACE * BLOCK_IN + at, N_SPACE, stride=BLOCK_IN), :]

        return unpack_row(get, q, BLOCK_IN, EXTRA_IN)

    def field_column(s, c):
        return jnp.concatenate([row(s, slot(of, c, r)) for of in range(2) for r in range(ROWS)], axis=0)

    other = 1 - segment

    def adjoint_row(at):
        return row(segment, N_FIELD + at) if at < OWN else row(other, N_FIELD + at - OWN)

    def adjoint_column(c):
        return jnp.concatenate([adjoint_row(slot(of, c, r)) for of in range(2) for r in range(ROWS)], axis=0)

    w_ref[pl.ds(pl.multiple_of(segment * 4 * CH, 8), 4 * CH), :] = own_w_ref[...]
    b_ref[segment] = own_b_ref[...]
    inside = lane_index(N_SPACE) < CH
    for n in range(4):
        b_ref[other, n : n + 1, :] = row(other, OFFSET_ROW + n)[:1]
    for j in range(SHARE):
        w_ref[pl.ds(other * 4 * CH + j, N_SPACE, stride=SHARE), :] = jnp.where(inside, row(other, WEIGHT_ROW + j), 0.0)

    nothing = jnp.zeros((H, LANES), F32)

    def block(value, n):
        return value[:, LANES * n : LANES * (n + 1)]

    def spread(first):
        one = jnp.concatenate([first[:H], jnp.where(is_special, nothing, first[H:])], axis=0)
        return [one, jnp.concatenate([first[H:], nothing], axis=0)]

    def ordinary(column):
        r, i = column[:H], column[H:]
        return [jnp.concatenate([r, i], axis=1), jnp.concatenate([r, -i], axis=1)]

    def leading(one, two):
        mirror = jnp.where(is_special, two, jnp.concatenate([one[:H], -one[H:]], axis=0))
        return [jnp.concatenate([v[:H], v[H:]], axis=1) for v in (one, mirror)]

    def transform(columns, parts):
        return product(table, cut(jnp.concatenate(columns, axis=1), parts), NN, parts)

    adjoint_first = adjoint_column(0)
    fields = transform(
        [v for s in range(2) for v in spread(field_column(s, 0)) + [field_column(s, 1), field_column(s, 2)]], 3
    )
    adjoints = transform(spread(adjoint_first) + [adjoint_column(1), adjoint_column(2)], 2)

    weights = []
    gap = jnp.zeros((LANES - CH, 2 * LANES), F32)
    for s in range(N_SEG):
        for n in range(2):
            real, imag = (w_ref[pl.ds((4 * s + 2 * n + of) * CH, CH), :] for of in range(2))
            top, bottom = jnp.concatenate([real, imag], axis=1), jnp.concatenate([-imag, real], axis=1)
            weights.append(thirds(jnp.concatenate([top, gap, bottom, gap], axis=0)))

    def offset(s, n):
        return jnp.concatenate([b_ref[s, 2 * n + of : 2 * n + of + 1, :] for of in range(2)], axis=1)

    forward = []
    for s in range(2):
        parts = [block(fields, 4 * s + n) for n in range(4)]
        x = jnp.concatenate(leading(parts[0], parts[1]) + ordinary(parts[2]) + ordinary(parts[3]), axis=0)
        x = thirds(x)
        hid = product(x, weights[2 * s], NN, 3) + offset(s, 0)
        act = thirds(jnp.maximum(hid, 0.0))
        out = product(act, weights[2 * s + 1], NN, 3) + offset(s, 1)
        forward.append((x, hid, act, out))

    def backward(s, upstream):
        x, hid, act, out = forward[s]
        grad_out = jnp.where(jnp.abs(out) > SHRINK, upstream, 0.0)
        grad_out_halves = halves(grad_out)
        grad_hid = jnp.where(hid > 0.0, product(grad_out_halves, weights[2 * s + 1], NT), 0.0)
        grad_hid_halves = halves(grad_hid)
        grad_x = product(grad_hid_halves, weights[2 * s], NT)
        pairs = []
        for n, (left, right) in enumerate(((x, grad_hid_halves), (act, grad_out_halves))):
            full = product(left, right, TN)
            grads_ref[pl.ds((2 * n) * CH, CH), :] = full[:CH, :LANES] + full[LANES : LANES + CH, LANES:]
            grads_ref[pl.ds((2 * n + 1) * CH, CH), :] = full[:CH, LANES:] - full[LANES : LANES + CH, :LANES]
        offsets = []
        for value in (grad_hid, grad_out):
            total = jnp.sum(value, axis=0, keepdims=True)
            offsets += [total[:, :LANES], total[:, LANES:]]
        sums = []
        for c in range(COLS):
            one, two = grad_x[2 * c * H : (2 * c + 1) * H], grad_x[(2 * c + 1) * H : (2 * c + 2) * H]
            sums.append((one[:, :LANES] + two[:, :LANES], one[:, LANES:] - two[:, LANES:]))
        one = jnp.concatenate(
            [
                jnp.where(is_special, grad_x[:H, :LANES], sums[0][0]),
                -jnp.where(is_special, grad_x[:H, LANES:], sums[0][1]),
            ],
            axis=0,
        )
        two = jnp.concatenate([grad_x[H : 2 * H, :LANES], -grad_x[H : 2 * H, LANES:]], axis=0)
        back = transform([one, two] + [jnp.concatenate([r, -i], axis=0) for r, i in sums[1:]], 2)
        columns = []
        for n in (0, 2, 3):
            low = -block(back, n)[H:]
            if n == 0:
                low = jnp.where(is_special, block(back, 1)[:H], low)
            columns.append(jnp.concatenate([block(back, n)[:H], low], axis=0))
        return columns, [jnp.concatenate(pair, axis=0) for pair in sums[1:]], offsets

    def emit(s, columns, offsets):
        values = {}
        for c in range(COLS):
            for of in range(2):
                for r in range(ROWS):
                    base = (of * ROWS + r) * N_SPACE
                    values[slot(of, c, r)] = columns[c][base : base + N_SPACE]
        for j in range(SHARE):
            values[N_FIELD + j] = grads_ref[pl.ds(j, N_SPACE, stride=SHARE), :]
        for j in range(4):
            values[N_FIELD + SHARE + j] = jnp.broadcast_to(offsets[j], (N_SPACE, LANES))

        def put(q, value):
            out_ref[pl.ds(s * N_SPACE * BLOCK_OUT + q, N_SPACE, stride=BLOCK_OUT), :] = value

        pack_rows(put, N_SPACE, values, BLOCK_OUT, EXTRA_OUT)

    parts = [block(adjoints, n) for n in range(4)]
    upstream = jnp.concatenate(leading(parts[0], parts[1]) + ordinary(parts[2]) + ordinary(parts[3]), axis=0)
    columns_one, sums, offsets = backward(1, upstream)
    emit(1, columns_one, offsets)

    lead = transform(spread(adjoint_first + scale * columns_one[0]), 2)
    upstream = jnp.concatenate(
        leading(block(lead, 0), block(lead, 1))
        + ordinary(parts[2] + 0.5 * sums[0])
        + ordinary(parts[3] + 0.5 * sums[1]),
        axis=0,
    )
    columns_zero, sums, offsets = backward(0, upstream)
    emit(0, [one + zero for one, zero in zip(columns_one, columns_zero)], offsets)


def total_kernel(got_ref, share_ref, offset_ref):
    total = got_ref[pl.ds(0, BLOCK_OUT), :]
    for d in range(1, N_DEST):
        total = total + got_ref[pl.ds(d * BLOCK_OUT, BLOCK_OUT), :]
    late = join_thirds([total[EXTRA_OUT * third : EXTRA_OUT * (third + 1)] for third in range(3)])
    early = BLOCK_OUT - N_FIELD
    for p in range(N_SPACE):
        share_ref[pl.ds(p * SHARE, early), :] = total[N_FIELD:BLOCK_OUT]
        share_ref[pl.ds(p * SHARE + early, SHARE - early), :] = late[: SHARE - early]
    offset_ref[...] = late[SHARE - early : EXTRA_OUT]


def after_kernel(got_ref, g_ref, pair_ref, out_ref):
    for j in range(ROWS // 2):
        rows = []
        for rr in range(2):
            for of in range(2):
                for c in range(COLS):
                    rows.append(got_ref[pl.ds(slot(of, c, 2 * j + rr), N_DEST, stride=BLOCK_OUT), :])
        spectrum = halves(jnp.concatenate(rows, axis=0))
        back = product(spectrum, [pair_ref[n] for n in range(2)], TN)
        lanes = pl.ds(2 * W * j, 2 * W)
        out_ref[:, lanes] = g_ref[:, lanes] + back[:CH]


def vmem(count):
    return [pl.BlockSpec(memory_space=pltpu.VMEM)] * count


PARAMS = pltpu.CompilerParams(vmem_limit_bytes=VMEM_LIMIT)


def shards(acts, cotangent, w_in, w_out, b_in, b_out):
    everyone = ("segment", "space")
    block_input, given = acts[0, 0], cotangent[0]

    by_owner = width_table().reshape(2, COLS, N_SEG, N_SPACE, W).transpose(2, 0, 1, 3, 4)
    table_parts = split_table(by_owner.reshape(N_SEG, 2 * COLS * N_SPACE, W), 3)
    pair_parts = split_table(row_pair_table(), 2)
    height_parts = split_table(height_table(), 3)

    given_arrays = (block_input, given, b_in[0], b_out[0], w_in[0, :, 0], w_out[0, :, 0], table_parts)
    copied = [(CH, ROWS * W), (CH, ROWS * W), (2, CH), (2, CH), (4, CH, CH)]
    sent = pl.pallas_call(
        ahead_kernel,
        out_shape=jax.ShapeDtypeStruct((N_DEST * BLOCK_IN, LANES), F32),
        in_specs=[pl.BlockSpec(memory_space=pl.ANY)] * len(given_arrays),
        out_specs=pl.BlockSpec(memory_space=pltpu.VMEM),
        scratch_shapes=[pltpu.VMEM(shape, F32) for shape in copied]
        + [pltpu.VMEM(table_parts.shape, BF16), pltpu.SemaphoreType.DMA((1 + ROWS + 4,))],
        compiler_params=pltpu.CompilerParams(vmem_limit_bytes=AHEAD_VMEM),
        name="ahead",
    )(*given_arrays)
    got = lax.all_to_all(sent.reshape(N_DEST, BLOCK_IN, 1, LANES), everyone, 0, 0, tiled=True)

    own_w = jnp.concatenate([w_in[0, :, 0], w_out[0, :, 0]])
    own_w = jnp.pad(own_w, ((0, 0), (0, 0), (0, LANES - CH))).reshape(4 * CH, LANES)
    own_b = jnp.pad(jnp.concatenate([b_in[0], b_out[0]]), ((0, 4), (0, LANES - CH)))

    sent = pl.pallas_call(
        middle_kernel,
        out_shape=jax.ShapeDtypeStruct((N_DEST * BLOCK_OUT, LANES), F32),
        in_specs=vmem(4),
        out_specs=pl.BlockSpec(memory_space=pltpu.VMEM),
        scratch_shapes=[
            pltpu.VMEM((4 * CH, LANES), F32),
            pltpu.VMEM((N_SEG * 4 * CH, LANES), F32),
            pltpu.VMEM((N_SEG, 8, LANES), F32),
        ],
        compiler_params=PARAMS,
        name="middle",
    )(got.reshape(N_DEST * BLOCK_IN, LANES), own_w, own_b, height_parts)
    got = lax.all_to_all(sent.reshape(N_DEST, BLOCK_OUT, LANES), everyone, 0, 0, tiled=True)
    got = got.reshape(N_DEST * BLOCK_OUT, LANES)

    mine, offsets = pl.pallas_call(
        total_kernel,
        out_shape=(
            jax.ShapeDtypeStruct((N_SPACE * SHARE, LANES), F32),
            jax.ShapeDtypeStruct((4, LANES), F32),
        ),
        in_specs=vmem(1),
        out_specs=tuple(vmem(2)),
        compiler_params=PARAMS,
        name="total",
    )(got)
    whole = lax.all_to_all(mine.reshape(N_SPACE, SHARE, LANES), "space", 0, 0, tiled=True)

    adjoint = pl.pallas_call(
        after_kernel,
        out_shape=jax.ShapeDtypeStruct((CH, ROWS * W), F32),
        in_specs=vmem(3),
        out_specs=pl.BlockSpec(memory_space=pltpu.VMEM),
        compiler_params=PARAMS,
        name="after",
    )(got, given, pair_parts)

    whole = whole.reshape(4, CH, LANES)[:, :, :CH]
    offsets = offsets[:, :CH]
    return (
        adjoint[None, None],
        whole[:2].reshape(w_in.shape),
        whole[2:].reshape(w_out.shape),
        offsets[:2].reshape(b_in.shape),
        offsets[2:].reshape(b_out.shape),
    )


def solution(mesh):
    placed = (
        P("segment", None, "chan", "space"),
        P(None, "chan", "space"),
        P("segment", None, "chan", None, None),
        P("segment", None, "chan", None, None),
        P("segment", None, "chan"),
        P("segment", None, "chan"),
    )
    return jax.shard_map(
        shards,
        mesh=mesh,
        in_specs=placed,
        out_specs=(
            P("segment", None, "chan", "space"),
            P("segment", None, "chan", None, None),
            P("segment", None, "chan", None, None),
            P("segment", None, "chan"),
            P("segment", None, "chan"),
        ),
        check_vma=False,
    )
```

```python
import math

import jax
import jax.numpy as jnp
import ml_dtypes
import numpy as np
from jax import lax
from jax.experimental import pallas as pl
from jax.experimental.pallas import tpu as pltpu
from jax.sharding import PartitionSpec as P

H = 96
W = 192
CH = 96
LANES = 128
N_SPACE = 16
N_SEG = 2
N_DEST = N_SPACE * N_SEG
ROWS = H // N_SPACE
COLS = W // 2 // N_DEST
BLOCK_IN, EXTRA_IN = 51, 17
BLOCK_OUT, EXTRA_OUT = 48, 16
SHRINK = 0.3
WIDE = 256
BF16 = jnp.bfloat16
F32 = jnp.float32
VMEM_LIMIT = 24 * 1024 * 1024
AHEAD_VMEM = 56 * 1024 * 1024


def split_table(table, count):
    parts = []
    for _ in range(count):
        parts.append(table.astype(np.float32).astype(ml_dtypes.bfloat16))
        table = table - parts[-1].astype(np.float64)
    return np.stack(parts)


def dft(length):
    index = np.arange(length)
    phase = 2.0 * math.pi * (np.outer(index, index) % length) / length
    return np.cos(phase) / math.sqrt(length), np.sin(phase) / math.sqrt(length)


def width_table():
    cos_w, sin_w = dft(W)
    half = W // 2
    real, imag = cos_w[:half].copy(), -sin_w[:half].copy()
    imag[0] = cos_w[half]
    both = np.stack([real, imag])
    return both.reshape(2, N_DEST, COLS, W).transpose(0, 2, 1, 3)


def height_table():
    cos_h, sin_h = dft(H)
    order = np.array([ROWS * p + r for r in range(ROWS) for p in range(N_SPACE)])
    cos_h, sin_h = cos_h[np.ix_(order, order)], sin_h[np.ix_(order, order)]
    return np.block([[cos_h, sin_h], [-sin_h, cos_h]])


def row_pair_table():
    flat = width_table().reshape(2 * COLS * N_DEST, W)
    zero = np.zeros_like(flat)
    return np.block([[flat, zero], [zero, flat]])


def cut(value, count):
    parts = []
    for n in range(count):
        parts.append(value.astype(BF16))
        if n < count - 1:
            value = value - parts[-1].astype(F32)
    return parts


def halves(value):
    return cut(value, 2)


def thirds(value):
    return cut(value, 3)


def terms(parts):
    return [(n, order - n) for order in reversed(range(parts)) for n in range(order + 1)]


def product(a, b, contract, parts=2):
    (left,), (right,) = contract
    if isinstance(a, list):
        a = jnp.concatenate([a[n] for n, _ in terms(parts)], axis=left)
    b = jnp.concatenate([b[n] for _, n in terms(parts)], axis=right)
    return lax.dot_general(a, b, (contract, ((), ())), preferred_element_type=F32)


def lay_out(split, parts, width):
    pad = [(0, 0)] * (split.ndim - 2) + [(0, width - split.shape[-1])]
    return np.concatenate([np.pad(split[n], pad) for n, _ in terms(parts)], axis=-1)


NN = ((1,), (0,))
NT = ((1,), (1,))
TN = ((0,), (0,))


def lane_index(rows):
    return lax.broadcasted_iota(jnp.int32, (rows, LANES), 1)


def slot(part, c, r):
    return (part * COLS + c) * ROWS + r


N_FIELD = 2 * COLS * ROWS
OWN = 32
OFFSET_ROW = 2 * N_FIELD - OWN
WEIGHT_ROW = OFFSET_ROW + 4
SHARE = 4 * CH // N_SPACE


def pack_rows(put, count, values, block, extras):
    lane = lane_index(count)
    for q in range(block):
        third, extra = divmod(q, extras)
        value = values[q]
        if third < 3:
            value = jnp.where(lane < CH, value, pltpu.roll(values[block + extra], CH - 32 * third, 1))
        put(q, value)


def join_thirds(thirds_of):
    lane = lane_index(thirds_of[0].shape[0])
    value = jnp.zeros(thirds_of[0].shape, F32)
    for third, part in enumerate(thirds_of):
        moved = pltpu.roll(part, (32 * third - CH) % LANES, 1)
        value = jnp.where((lane >= 32 * third) & (lane < 32 * third + 32), moved, value)
    return value


def unpack_row(get, q, block, extras):
    if q < block:
        return get(q)
    return join_thirds([get(q - block + extras * third) for third in range(3)])


def ahead_kernel(
    x_hbm, g_hbm, b_in_hbm, b_out_hbm, w_in_hbm, w_out_hbm, table_hbm,
    out_hbm, x_ref, g_ref, b_in_ref, b_out_ref, w_ref, table_ref, out_ref, sems,
):
    segment, space = lax.axis_index("segment"), lax.axis_index("space")
    pairs = [(table_hbm, table_ref)]
    for src, dst in ((x_hbm, x_ref), (g_hbm, g_ref)):
        dst[:, pl.ds(ROWS * W, LANES)] = jnp.zeros((CH, LANES), F32)
        for j in range(ROWS // 2):
            lanes = pl.ds(2 * W * j, 2 * W)
            pairs.append((src.at[:, lanes], dst.at[:, lanes]))
    pairs += [(b_in_hbm, b_in_ref), (b_out_hbm, b_out_ref), (w_in_hbm, w_ref.at[0:2]), (w_out_hbm, w_ref.at[2:4])]
    copies = [pltpu.make_async_copy(src, dst, sems.at[n]) for n, (src, dst) in enumerate(pairs)]
    for copy in copies:
        copy.start()
    pad = jnp.zeros((LANES - CH, WIDE), F32)
    fields = [{} for _ in range(N_SEG)]
    adjoints = {}

    def two_rows(ref, r):
        return jnp.concatenate([ref[:, pl.ds(W * r, WIDE)], pad, ref[:, pl.ds(W * (r + 1), WIDE)], pad], axis=0)

    def cut_out(value, base, rr):
        return value[base : base + N_SPACE, LANES * rr : LANES * (rr + 1)]

    copies[0].wait()
    table = table_ref[...].reshape(N_SEG * 2 * COLS * N_SPACE, 6 * WIDE)
    last = (2 * COLS - 1) * N_SPACE
    short = pl.ds(3 * WIDE, 3 * WIDE)
    part = jnp.concatenate([table_ref[segment, :, short], table_ref[1 - segment, last:, short]], axis=0)
    others = {}
    for r in range(0, ROWS, 2):
        if r == 0:
            copies[1].wait()
        if r + 2 < ROWS:
            copies[2 + r // 2].wait()
        field = product(table, thirds(two_rows(x_ref, r)), NT, 3)
        for rr in range(2):
            for s in range(N_SEG):
                for of in range(2):
                    for c in range(COLS):
                        fields[s][slot(of, c, r + rr)] = cut_out(field, ((s * 2 + of) * COLS + c) * N_SPACE, rr)
    for r in range(0, ROWS, 2):
        if r == 0:
            copies[1 + ROWS // 2].wait()
        if r + 2 < ROWS:
            copies[2 + ROWS // 2 + r // 2].wait()
        adjoint = product(part, halves(two_rows(g_ref, r)), NT)
        for rr in range(2):
            for of in range(2):
                for c in range(COLS):
                    at = slot(of, c, r + rr)
                    if at < OWN:
                        adjoints[N_FIELD + at] = cut_out(adjoint, (of * COLS + c) * N_SPACE, rr)
                    else:
                        others[N_FIELD + at - OWN] = cut_out(adjoint, last + N_SPACE, rr)
    for copy in copies[1 + ROWS :]:
        copy.wait()

    def to_all(row):
        return jnp.broadcast_to(row, (N_SPACE, LANES))

    fill = jnp.zeros((1, LANES - CH), F32)
    for n, ref in enumerate((b_in_ref, b_out_ref)):
        for of in range(2):
            others[OFFSET_ROW + 2 * n + of] = to_all(jnp.concatenate([ref[of : of + 1, :], fill], axis=1))
    start = pl.multiple_of(lax.rem(space, 4) * SHARE, 8)
    weights = w_ref[space // 4, pl.ds(start, SHARE), :]
    weights = jnp.concatenate([weights, jnp.zeros((SHARE, LANES - CH), F32)], axis=1)
    for j in range(SHARE):
        others[WEIGHT_ROW + j] = to_all(weights[j : j + 1])

    sends = []
    for s in range(N_SEG):
        values = dict(fields[s])
        for q in range(N_FIELD, N_FIELD + OWN):
            values[q] = jnp.where(segment == s, adjoints[q], others[q])

        def put(q, value, s=s):
            out_ref[pl.ds(s * N_SPACE * BLOCK_IN + q, N_SPACE, stride=BLOCK_IN), :] = value

        pack_rows(put, N_SPACE, values, BLOCK_IN, EXTRA_IN)
        half = pl.ds(s * N_SPACE * BLOCK_IN, N_SPACE * BLOCK_IN)
        sends.append(pltpu.make_async_copy(out_ref.at[half], out_hbm.at[half], sems.at[len(copies) + s]))
        sends[-1].start()
    for send in sends:
        send.wait()


def middle_kernel(got_ref, own_w_ref, own_b_ref, long_ref, short_ref, out_ref, grads_ref, w_ref, b_ref):
    segment, space = lax.axis_index("segment"), lax.axis_index("space")
    is_special = (segment == 0) & (space == 0)
    scale = jnp.where(is_special, 1.0, 0.5).astype(F32)

    def row(source, q):
        def get(at):
            return got_ref[pl.ds(source * N_SPACE * BLOCK_IN + at, N_SPACE, stride=BLOCK_IN), :]

        return unpack_row(get, q, BLOCK_IN, EXTRA_IN)

    def field_column(s, c):
        return jnp.concatenate([row(s, slot(of, c, r)) for of in range(2) for r in range(ROWS)], axis=0)

    other = 1 - segment

    def adjoint_row(at):
        return row(segment, N_FIELD + at) if at < OWN else row(other, N_FIELD + at - OWN)

    def adjoint_column(c):
        return jnp.concatenate([adjoint_row(slot(of, c, r)) for of in range(2) for r in range(ROWS)], axis=0)

    w_ref[pl.ds(pl.multiple_of(segment * 4 * CH, 8), 4 * CH), :] = own_w_ref[...]
    b_ref[segment] = own_b_ref[...]
    inside = lane_index(N_SPACE) < CH
    for n in range(4):
        b_ref[other, n : n + 1, :] = row(other, OFFSET_ROW + n)[:1]
    for j in range(SHARE):
        w_ref[pl.ds(other * 4 * CH + j, N_SPACE, stride=SHARE), :] = jnp.where(inside, row(other, WEIGHT_ROW + j), 0.0)

    nothing = jnp.zeros((H, LANES), F32)

    def block(value, n):
        return value[:, LANES * n : LANES * (n + 1)]

    def spread(first):
        one = jnp.concatenate([first[:H], jnp.where(is_special, nothing, first[H:])], axis=0)
        return [one, jnp.concatenate([first[H:], nothing], axis=0)]

    def ordinary(column):
        r, i = column[:H], column[H:]
        return [jnp.concatenate([r, i], axis=1), jnp.concatenate([r, -i], axis=1)]

    def leading(one, two):
        mirror = jnp.where(is_special, two, jnp.concatenate([one[:H], -one[H:]], axis=0))
        return [jnp.concatenate([v[:H], v[H:]], axis=1) for v in (one, mirror)]

    def transform(columns, parts):
        table = long_ref[...] if parts == 3 else short_ref[...]
        return product(table, cut(jnp.concatenate(columns, axis=1), parts), NN, parts)

    adjoint_first = adjoint_column(0)
    fields = transform(
        [v for s in range(2) for v in spread(field_column(s, 0)) + [field_column(s, 1), field_column(s, 2)]], 3
    )
    adjoints = transform(spread(adjoint_first) + [adjoint_column(1), adjoint_column(2)], 2)

    weights = []
    gap = jnp.zeros((LANES - CH, 2 * LANES), F32)
    for s in range(N_SEG):
        for n in range(2):
            real, imag = (w_ref[pl.ds((4 * s + 2 * n + of) * CH, CH), :] for of in range(2))
            top, bottom = jnp.concatenate([real, imag], axis=1), jnp.concatenate([-imag, real], axis=1)
            weights.append(thirds(jnp.concatenate([top, gap, bottom, gap], axis=0)))

    def offset(s, n):
        return jnp.concatenate([b_ref[s, 2 * n + of : 2 * n + of + 1, :] for of in range(2)], axis=1)

    forward = []
    for s in range(2):
        parts = [block(fields, 4 * s + n) for n in range(4)]
        x = jnp.concatenate(leading(parts[0], parts[1]) + ordinary(parts[2]) + ordinary(parts[3]), axis=0)
        x = thirds(x)
        hid = product(x, weights[2 * s], NN, 3) + offset(s, 0)
        act = thirds(jnp.maximum(hid, 0.0))
        out = product(act, weights[2 * s + 1], NN, 3) + offset(s, 1)
        forward.append((x, hid, act, out))

    def backward(s, upstream):
        x, hid, act, out = forward[s]
        grad_out = jnp.where(jnp.abs(out) > SHRINK, upstream, 0.0)
        grad_out_halves = halves(grad_out)
        grad_hid = jnp.where(hid > 0.0, product(grad_out_halves, weights[2 * s + 1], NT), 0.0)
        grad_hid_halves = halves(grad_hid)
        grad_x = product(grad_hid_halves, weights[2 * s], NT)
        pairs = []
        for n, (left, right) in enumerate(((x, grad_hid_halves), (act, grad_out_halves))):
            full = product(left, right, TN)
            grads_ref[pl.ds((2 * n) * CH, CH), :] = full[:CH, :LANES] + full[LANES : LANES + CH, LANES:]
            grads_ref[pl.ds((2 * n + 1) * CH, CH), :] = full[:CH, LANES:] - full[LANES : LANES + CH, :LANES]
        offsets = []
        for value in (grad_hid, grad_out):
            total = jnp.sum(value, axis=0, keepdims=True)
            offsets += [total[:, :LANES], total[:, LANES:]]
        sums = []
        for c in range(COLS):
            one, two = grad_x[2 * c * H : (2 * c + 1) * H], grad_x[(2 * c + 1) * H : (2 * c + 2) * H]
            sums.append((one[:, :LANES] + two[:, :LANES], one[:, LANES:] - two[:, LANES:]))
        one = jnp.concatenate(
            [
                jnp.where(is_special, grad_x[:H, :LANES], sums[0][0]),
                -jnp.where(is_special, grad_x[:H, LANES:], sums[0][1]),
            ],
            axis=0,
        )
        two = jnp.concatenate([grad_x[H : 2 * H, :LANES], -grad_x[H : 2 * H, LANES:]], axis=0)
        back = transform([one, two] + [jnp.concatenate([r, -i], axis=0) for r, i in sums[1:]], 2)
        columns = []
        for n in (0, 2, 3):
            low = -block(back, n)[H:]
            if n == 0:
                low = jnp.where(is_special, block(back, 1)[:H], low)
            columns.append(jnp.concatenate([block(back, n)[:H], low], axis=0))
        return columns, [jnp.concatenate(pair, axis=0) for pair in sums[1:]], offsets

    def emit(s, columns, offsets):
        values = {}
        for c in range(COLS):
            for of in range(2):
                for r in range(ROWS):
                    base = (of * ROWS + r) * N_SPACE
                    values[slot(of, c, r)] = columns[c][base : base + N_SPACE]
        for j in range(SHARE):
            values[N_FIELD + j] = grads_ref[pl.ds(j, N_SPACE, stride=SHARE), :]
        for j in range(4):
            values[N_FIELD + SHARE + j] = jnp.broadcast_to(offsets[j], (N_SPACE, LANES))

        def put(q, value):
            out_ref[pl.ds(s * N_SPACE * BLOCK_OUT + q, N_SPACE, stride=BLOCK_OUT), :] = value

        pack_rows(put, N_SPACE, values, BLOCK_OUT, EXTRA_OUT)

    parts = [block(adjoints, n) for n in range(4)]
    upstream = jnp.concatenate(leading(parts[0], parts[1]) + ordinary(parts[2]) + ordinary(parts[3]), axis=0)
    columns_one, sums, offsets = backward(1, upstream)
    emit(1, columns_one, offsets)

    lead = transform(spread(adjoint_first + scale * columns_one[0]), 2)
    upstream = jnp.concatenate(
        leading(block(lead, 0), block(lead, 1))
        + ordinary(parts[2] + 0.5 * sums[0])
        + ordinary(parts[3] + 0.5 * sums[1]),
        axis=0,
    )
    columns_zero, sums, offsets = backward(0, upstream)
    emit(0, [one + zero for one, zero in zip(columns_one, columns_zero)], offsets)


def total_kernel(got_ref, share_ref, offset_ref):
    total = got_ref[pl.ds(0, BLOCK_OUT), :]
    for d in range(1, N_DEST):
        total = total + got_ref[pl.ds(d * BLOCK_OUT, BLOCK_OUT), :]
    late = join_thirds([total[EXTRA_OUT * third : EXTRA_OUT * (third + 1)] for third in range(3)])
    early = BLOCK_OUT - N_FIELD
    for p in range(N_SPACE):
        share_ref[pl.ds(p * SHARE, early), :] = total[N_FIELD:BLOCK_OUT]
        share_ref[pl.ds(p * SHARE + early, SHARE - early), :] = late[: SHARE - early]
    offset_ref[...] = late[SHARE - early : EXTRA_OUT]


def after_kernel(got_ref, g_ref, pair_ref, out_ref):
    for j in range(ROWS // 2):
        rows = []
        for rr in range(2):
            for of in range(2):
                for c in range(COLS):
                    rows.append(got_ref[pl.ds(slot(of, c, 2 * j + rr), N_DEST, stride=BLOCK_OUT), :])
        spectrum = halves(jnp.concatenate(rows, axis=0))
        back = product(spectrum, [pair_ref[n] for n in range(2)], TN)
        lanes = pl.ds(2 * W * j, 2 * W)
        out_ref[:, lanes] = g_ref[:, lanes] + back[:CH]


def vmem(count):
    return [pl.BlockSpec(memory_space=pltpu.VMEM)] * count


PARAMS = pltpu.CompilerParams(vmem_limit_bytes=VMEM_LIMIT)


def shards(acts, cotangent, w_in, w_out, b_in, b_out):
    everyone = ("segment", "space")
    block_input, given = acts[0, 0], cotangent[0]

    by_owner = width_table().reshape(2, COLS, N_SEG, N_SPACE, W).transpose(2, 0, 1, 3, 4)
    width_parts = split_table(by_owner.reshape(N_SEG, 2 * COLS * N_SPACE, W), 3)
    width_terms = lay_out(width_parts, 3, WIDE)
    pair_parts = split_table(row_pair_table(), 2)
    height_parts = split_table(height_table(), 3)
    height_terms = [lay_out(height_parts, parts, 2 * H) for parts in (3, 2)]

    given_arrays = (block_input, given, b_in[0], b_out[0], w_in[0, :, 0], w_out[0, :, 0], width_terms)
    copied = [(CH, ROWS * W + LANES), (CH, ROWS * W + LANES), (2, CH), (2, CH), (4, CH, CH)]
    sent = pl.pallas_call(
        ahead_kernel,
        out_shape=jax.ShapeDtypeStruct((N_DEST * BLOCK_IN, LANES), F32),
        in_specs=[pl.BlockSpec(memory_space=pl.ANY)] * len(given_arrays),
        out_specs=pl.BlockSpec(memory_space=pl.ANY),
        scratch_shapes=[pltpu.VMEM(shape, F32) for shape in copied]
        + [
            pltpu.VMEM(width_terms.shape, BF16),
            pltpu.VMEM((N_DEST * BLOCK_IN, LANES), F32),
            pltpu.SemaphoreType.DMA((1 + ROWS + 4 + N_SEG,)),
        ],
        compiler_params=pltpu.CompilerParams(vmem_limit_bytes=AHEAD_VMEM),
        name="ahead",
    )(*given_arrays)
    got = lax.all_to_all(sent.reshape(N_DEST, BLOCK_IN, 1, LANES), everyone, 0, 0, tiled=True)

    own_w = jnp.concatenate([w_in[0, :, 0], w_out[0, :, 0]])
    own_w = jnp.pad(own_w, ((0, 0), (0, 0), (0, LANES - CH))).reshape(4 * CH, LANES)
    own_b = jnp.pad(jnp.concatenate([b_in[0], b_out[0]]), ((0, 4), (0, LANES - CH)))

    sent = pl.pallas_call(
        middle_kernel,
        out_shape=jax.ShapeDtypeStruct((N_DEST * BLOCK_OUT, LANES), F32),
        in_specs=vmem(5),
        out_specs=pl.BlockSpec(memory_space=pltpu.VMEM),
        scratch_shapes=[
            pltpu.VMEM((4 * CH, LANES), F32),
            pltpu.VMEM((N_SEG * 4 * CH, LANES), F32),
            pltpu.VMEM((N_SEG, 8, LANES), F32),
        ],
        compiler_params=PARAMS,
        name="middle",
    )(got.reshape(N_DEST * BLOCK_IN, LANES), own_w, own_b, *height_terms)
    got = lax.all_to_all(sent.reshape(N_DEST, BLOCK_OUT, LANES), everyone, 0, 0, tiled=True)
    got = got.reshape(N_DEST * BLOCK_OUT, LANES)

    mine, offsets = pl.pallas_call(
        total_kernel,
        out_shape=(
            jax.ShapeDtypeStruct((N_SPACE * SHARE, LANES), F32),
            jax.ShapeDtypeStruct((4, LANES), F32),
        ),
        in_specs=vmem(1),
        out_specs=tuple(vmem(2)),
        compiler_params=PARAMS,
        name="total",
    )(got)
    whole = lax.all_to_all(mine.reshape(N_SPACE, SHARE, LANES), "space", 0, 0, tiled=True)

    adjoint = pl.pallas_call(
        after_kernel,
        out_shape=jax.ShapeDtypeStruct((CH, ROWS * W), F32),
        in_specs=vmem(3),
        out_specs=pl.BlockSpec(memory_space=pltpu.VMEM),
        compiler_params=PARAMS,
        name="after",
    )(got, given, pair_parts)

    whole = whole.reshape(4, CH, LANES)[:, :, :CH]
    offsets = offsets[:, :CH]
    return (
        adjoint[None, None],
        whole[:2].reshape(w_in.shape),
        whole[2:].reshape(w_out.shape),
        offsets[:2].reshape(b_in.shape),
        offsets[2:].reshape(b_out.shape),
    )


def solution(mesh):
    placed = (
        P("segment", None, "chan", "space"),
        P(None, "chan", "space"),
        P("segment", None, "chan", None, None),
        P("segment", None, "chan", None, None),
        P("segment", None, "chan"),
        P("segment", None, "chan"),
    )
    return jax.shard_map(
        shards,
        mesh=mesh,
        in_specs=placed,
        out_specs=(
            P("segment", None, "chan", "space"),
            P("segment", None, "chan", None, None),
            P("segment", None, "chan", None, None),
            P("segment", None, "chan"),
            P("segment", None, "chan"),
        ),
        check_vma=False,
    )
```

```python
import math

import jax
import jax.numpy as jnp
import ml_dtypes
import numpy as np
from jax import lax
from jax.experimental import pallas as pl
from jax.experimental.pallas import tpu as pltpu
from jax.sharding import PartitionSpec as P

H = 96
W = 192
CH = 96
LANES = 128
N_SPACE = 16
N_SEG = 2
N_DEST = N_SPACE * N_SEG
ROWS = H // N_SPACE
COLS = W // 2 // N_DEST
BLOCK_IN, EXTRA_IN = 51, 17
BLOCK_OUT, EXTRA_OUT = 48, 16
SHRINK = 0.3
WIDE = 256
BF16 = jnp.bfloat16
F32 = jnp.float32
VMEM_LIMIT = 24 * 1024 * 1024
AHEAD_VMEM = 56 * 1024 * 1024


def split_table(table, count):
    parts = []
    for _ in range(count):
        parts.append(table.astype(np.float32).astype(ml_dtypes.bfloat16))
        table = table - parts[-1].astype(np.float64)
    return np.stack(parts)


def dft(length):
    index = np.arange(length)
    phase = 2.0 * math.pi * (np.outer(index, index) % length) / length
    return np.cos(phase) / math.sqrt(length), np.sin(phase) / math.sqrt(length)


def width_table():
    cos_w, sin_w = dft(W)
    half = W // 2
    real, imag = cos_w[:half].copy(), -sin_w[:half].copy()
    imag[0] = cos_w[half]
    both = np.stack([real, imag])
    return both.reshape(2, N_DEST, COLS, W).transpose(0, 2, 1, 3)


def height_table():
    cos_h, sin_h = dft(H)
    order = np.array([ROWS * p + r for r in range(ROWS) for p in range(N_SPACE)])
    cos_h, sin_h = cos_h[np.ix_(order, order)], sin_h[np.ix_(order, order)]
    return np.block([[cos_h, sin_h], [-sin_h, cos_h]])


def row_pair_table():
    flat = width_table().reshape(2 * COLS * N_DEST, W)
    zero = np.zeros_like(flat)
    return np.block([[flat, zero], [zero, flat]])


def cut(value, count):
    parts = []
    for n in range(count):
        parts.append(value.astype(BF16))
        if n < count - 1:
            value = value - parts[-1].astype(F32)
    return parts


def halves(value):
    return cut(value, 2)


def thirds(value):
    return cut(value, 3)


def terms(parts):
    return [(n, order - n) for order in reversed(range(parts)) for n in range(order + 1)]


def product(a, b, contract, parts=2):
    (left,), (right,) = contract
    if isinstance(a, list):
        a = jnp.concatenate([a[n] for n, _ in terms(parts)], axis=left)
    b = jnp.concatenate([b[n] for _, n in terms(parts)], axis=right)
    return lax.dot_general(a, b, (contract, ((), ())), preferred_element_type=F32)


def lay_out(split, parts, width):
    pad = [(0, 0)] * (split.ndim - 2) + [(0, width - split.shape[-1])]
    return np.concatenate([np.pad(split[n], pad) for n, _ in terms(parts)], axis=-1)


NN = ((1,), (0,))
NT = ((1,), (1,))
TN = ((0,), (0,))


def lane_index(rows):
    return lax.broadcasted_iota(jnp.int32, (rows, LANES), 1)


def slot(part, c, r):
    return (part * COLS + c) * ROWS + r


N_FIELD = 2 * COLS * ROWS
OWN = 32
OFFSET_ROW = 2 * N_FIELD - OWN
WEIGHT_ROW = OFFSET_ROW + 4
SHARE = 4 * CH // N_SPACE


def pack_rows(put, count, values, block, extras):
    lane = lane_index(count)
    for q in range(block):
        third, extra = divmod(q, extras)
        value = values[q]
        if third < 3:
            value = jnp.where(lane < CH, value, pltpu.roll(values[block + extra], CH - 32 * third, 1))
        put(q, value)


def join_thirds(thirds_of):
    lane = lane_index(thirds_of[0].shape[0])
    value = jnp.zeros(thirds_of[0].shape, F32)
    for third, part in enumerate(thirds_of):
        moved = pltpu.roll(part, (32 * third - CH) % LANES, 1)
        value = jnp.where((lane >= 32 * third) & (lane < 32 * third + 32), moved, value)
    return value


def unpack_row(get, q, block, extras):
    if q < block:
        return get(q)
    return join_thirds([get(q - block + extras * third) for third in range(3)])


def ahead_kernel(
    x_hbm, g_hbm, b_in_hbm, b_out_hbm, w_in_hbm, w_out_hbm, table_hbm,
    out_hbm, x_ref, g_ref, b_in_ref, b_out_ref, w_ref, table_ref, out_ref, sems,
):
    segment, space = lax.axis_index("segment"), lax.axis_index("space")
    pairs = [(table_hbm, table_ref)]
    for src, dst in ((x_hbm, x_ref), (g_hbm, g_ref)):
        dst[:, pl.ds(ROWS * W, LANES)] = jnp.zeros((CH, LANES), F32)
        for j in range(ROWS // 2):
            lanes = pl.ds(2 * W * j, 2 * W)
            pairs.append((src.at[:, lanes], dst.at[:, lanes]))
    pairs += [(b_in_hbm, b_in_ref), (b_out_hbm, b_out_ref), (w_in_hbm, w_ref.at[0:2]), (w_out_hbm, w_ref.at[2:4])]
    copies = [pltpu.make_async_copy(src, dst, sems.at[n]) for n, (src, dst) in enumerate(pairs)]
    for copy in copies:
        copy.start()
    pad = jnp.zeros((LANES - CH, WIDE), F32)
    fields = [{} for _ in range(N_SEG)]
    adjoints = {}

    def all_rows(ref):
        return jnp.concatenate(
            [piece for r in range(ROWS) for piece in (ref[:, pl.ds(W * r, WIDE)], pad)], axis=0
        )

    def cut_out(value, base, r):
        return value[base : base + N_SPACE, LANES * r : LANES * (r + 1)]

    copies[0].wait()
    table = table_ref[...].reshape(N_SEG * 2 * COLS * N_SPACE, 6 * WIDE)
    last = (2 * COLS - 1) * N_SPACE
    short = pl.ds(3 * WIDE, 3 * WIDE)
    part = jnp.concatenate([table_ref[segment, :, short], table_ref[1 - segment, last:, short]], axis=0)
    others = {}
    for copy in copies[1 : 1 + ROWS // 2]:
        copy.wait()
    field = product(table, thirds(all_rows(x_ref)), NT, 3)
    for copy in copies[1 + ROWS // 2 : 1 + ROWS]:
        copy.wait()
    adjoint = product(part, halves(all_rows(g_ref)), NT)
    for r in range(ROWS):
        for of in range(2):
            for c in range(COLS):
                at = slot(of, c, r)
                for s in range(N_SEG):
                    fields[s][at] = cut_out(field, ((s * 2 + of) * COLS + c) * N_SPACE, r)
                if at < OWN:
                    adjoints[N_FIELD + at] = cut_out(adjoint, (of * COLS + c) * N_SPACE, r)
                else:
                    others[N_FIELD + at - OWN] = cut_out(adjoint, last + N_SPACE, r)
    for copy in copies[1 + ROWS :]:
        copy.wait()

    def to_all(row):
        return jnp.broadcast_to(row, (N_SPACE, LANES))

    fill = jnp.zeros((1, LANES - CH), F32)
    for n, ref in enumerate((b_in_ref, b_out_ref)):
        for of in range(2):
            others[OFFSET_ROW + 2 * n + of] = to_all(jnp.concatenate([ref[of : of + 1, :], fill], axis=1))
    start = pl.multiple_of(lax.rem(space, 4) * SHARE, 8)
    weights = w_ref[space // 4, pl.ds(start, SHARE), :]
    weights = jnp.concatenate([weights, jnp.zeros((SHARE, LANES - CH), F32)], axis=1)
    for j in range(SHARE):
        others[WEIGHT_ROW + j] = to_all(weights[j : j + 1])

    sends = []
    for s in range(N_SEG):
        values = dict(fields[s])
        for q in range(N_FIELD, N_FIELD + OWN):
            values[q] = jnp.where(segment == s, adjoints[q], others[q])

        def put(q, value, s=s):
            out_ref[pl.ds(s * N_SPACE * BLOCK_IN + q, N_SPACE, stride=BLOCK_IN), :] = value

        pack_rows(put, N_SPACE, values, BLOCK_IN, EXTRA_IN)
        half = pl.ds(s * N_SPACE * BLOCK_IN, N_SPACE * BLOCK_IN)
        sends.append(pltpu.make_async_copy(out_ref.at[half], out_hbm.at[half], sems.at[len(copies) + s]))
        sends[-1].start()
    for send in sends:
        send.wait()


def middle_kernel(got_ref, own_w_ref, own_b_ref, long_ref, short_ref, out_ref, grads_ref, w_ref, b_ref):
    segment, space = lax.axis_index("segment"), lax.axis_index("space")
    is_special = (segment == 0) & (space == 0)
    scale = jnp.where(is_special, 1.0, 0.5).astype(F32)

    def row(source, q):
        def get(at):
            return got_ref[pl.ds(source * N_SPACE * BLOCK_IN + at, N_SPACE, stride=BLOCK_IN), :]

        return unpack_row(get, q, BLOCK_IN, EXTRA_IN)

    def field_column(s, c):
        return jnp.concatenate([row(s, slot(of, c, r)) for of in range(2) for r in range(ROWS)], axis=0)

    other = 1 - segment

    def adjoint_row(at):
        return row(segment, N_FIELD + at) if at < OWN else row(other, N_FIELD + at - OWN)

    def adjoint_column(c):
        return jnp.concatenate([adjoint_row(slot(of, c, r)) for of in range(2) for r in range(ROWS)], axis=0)

    w_ref[pl.ds(pl.multiple_of(segment * 4 * CH, 8), 4 * CH), :] = own_w_ref[...]
    b_ref[segment] = own_b_ref[...]
    inside = lane_index(N_SPACE) < CH
    for n in range(4):
        b_ref[other, n : n + 1, :] = row(other, OFFSET_ROW + n)[:1]
    for j in range(SHARE):
        w_ref[pl.ds(other * 4 * CH + j, N_SPACE, stride=SHARE), :] = jnp.where(inside, row(other, WEIGHT_ROW + j), 0.0)

    nothing = jnp.zeros((H, LANES), F32)

    def block(value, n):
        return value[:, LANES * n : LANES * (n + 1)]

    def spread(first):
        one = jnp.concatenate([first[:H], jnp.where(is_special, nothing, first[H:])], axis=0)
        return [one, jnp.concatenate([first[H:], nothing], axis=0)]

    def ordinary(column):
        r, i = column[:H], column[H:]
        return [jnp.concatenate([r, i], axis=1), jnp.concatenate([r, -i], axis=1)]

    def leading(one, two):
        mirror = jnp.where(is_special, two, jnp.concatenate([one[:H], -one[H:]], axis=0))
        return [jnp.concatenate([v[:H], v[H:]], axis=1) for v in (one, mirror)]

    def transform(columns, parts):
        table = long_ref[...] if parts == 3 else short_ref[...]
        return product(table, cut(jnp.concatenate(columns, axis=1), parts), NN, parts)

    adjoint_first = adjoint_column(0)
    fields = transform(
        [v for s in range(2) for v in spread(field_column(s, 0)) + [field_column(s, 1), field_column(s, 2)]], 3
    )
    adjoints = transform(spread(adjoint_first) + [adjoint_column(1), adjoint_column(2)], 2)

    weights = []
    gap = jnp.zeros((LANES - CH, 2 * LANES), F32)
    for s in range(N_SEG):
        for n in range(2):
            real, imag = (w_ref[pl.ds((4 * s + 2 * n + of) * CH, CH), :] for of in range(2))
            top, bottom = jnp.concatenate([real, imag], axis=1), jnp.concatenate([-imag, real], axis=1)
            weights.append(thirds(jnp.concatenate([top, gap, bottom, gap], axis=0)))

    def offset(s, n):
        return jnp.concatenate([b_ref[s, 2 * n + of : 2 * n + of + 1, :] for of in range(2)], axis=1)

    forward = []
    for s in range(2):
        parts = [block(fields, 4 * s + n) for n in range(4)]
        x = jnp.concatenate(leading(parts[0], parts[1]) + ordinary(parts[2]) + ordinary(parts[3]), axis=0)
        x = thirds(x)
        hid = product(x, weights[2 * s], NN, 3) + offset(s, 0)
        act = thirds(jnp.maximum(hid, 0.0))
        out = product(act, weights[2 * s + 1], NN, 3) + offset(s, 1)
        forward.append((x, hid, act, out))

    def backward(s, upstream):
        x, hid, act, out = forward[s]
        grad_out = jnp.where(jnp.abs(out) > SHRINK, upstream, 0.0)
        grad_out_halves = halves(grad_out)
        grad_hid = jnp.where(hid > 0.0, product(grad_out_halves, weights[2 * s + 1], NT), 0.0)
        grad_hid_halves = halves(grad_hid)
        grad_x = product(grad_hid_halves, weights[2 * s], NT)
        pairs = []
        for n, (left, right) in enumerate(((x, grad_hid_halves), (act, grad_out_halves))):
            full = product(left, right, TN)
            grads_ref[pl.ds((2 * n) * CH, CH), :] = full[:CH, :LANES] + full[LANES : LANES + CH, LANES:]
            grads_ref[pl.ds((2 * n + 1) * CH, CH), :] = full[:CH, LANES:] - full[LANES : LANES + CH, :LANES]
        offsets = []
        for value in (grad_hid, grad_out):
            total = jnp.sum(value, axis=0, keepdims=True)
            offsets += [total[:, :LANES], total[:, LANES:]]
        sums = []
        for c in range(COLS):
            one, two = grad_x[2 * c * H : (2 * c + 1) * H], grad_x[(2 * c + 1) * H : (2 * c + 2) * H]
            sums.append((one[:, :LANES] + two[:, :LANES], one[:, LANES:] - two[:, LANES:]))
        one = jnp.concatenate(
            [
                jnp.where(is_special, grad_x[:H, :LANES], sums[0][0]),
                -jnp.where(is_special, grad_x[:H, LANES:], sums[0][1]),
            ],
            axis=0,
        )
        two = jnp.concatenate([grad_x[H : 2 * H, :LANES], -grad_x[H : 2 * H, LANES:]], axis=0)
        back = transform([one, two] + [jnp.concatenate([r, -i], axis=0) for r, i in sums[1:]], 2)
        columns = []
        for n in (0, 2, 3):
            low = -block(back, n)[H:]
            if n == 0:
                low = jnp.where(is_special, block(back, 1)[:H], low)
            columns.append(jnp.concatenate([block(back, n)[:H], low], axis=0))
        return columns, [jnp.concatenate(pair, axis=0) for pair in sums[1:]], offsets

    def emit(s, columns, offsets):
        values = {}
        for c in range(COLS):
            for of in range(2):
                for r in range(ROWS):
                    base = (of * ROWS + r) * N_SPACE
                    values[slot(of, c, r)] = columns[c][base : base + N_SPACE]
        for j in range(SHARE):
            values[N_FIELD + j] = grads_ref[pl.ds(j, N_SPACE, stride=SHARE), :]
        for j in range(4):
            values[N_FIELD + SHARE + j] = jnp.broadcast_to(offsets[j], (N_SPACE, LANES))

        def put(q, value):
            out_ref[pl.ds(s * N_SPACE * BLOCK_OUT + q, N_SPACE, stride=BLOCK_OUT), :] = value

        pack_rows(put, N_SPACE, values, BLOCK_OUT, EXTRA_OUT)

    parts = [block(adjoints, n) for n in range(4)]
    upstream = jnp.concatenate(leading(parts[0], parts[1]) + ordinary(parts[2]) + ordinary(parts[3]), axis=0)
    columns_one, sums, offsets = backward(1, upstream)
    emit(1, columns_one, offsets)

    lead = transform(spread(adjoint_first + scale * columns_one[0]), 2)
    upstream = jnp.concatenate(
        leading(block(lead, 0), block(lead, 1))
        + ordinary(parts[2] + 0.5 * sums[0])
        + ordinary(parts[3] + 0.5 * sums[1]),
        axis=0,
    )
    columns_zero, sums, offsets = backward(0, upstream)
    emit(0, [one + zero for one, zero in zip(columns_one, columns_zero)], offsets)


def total_kernel(got_ref, share_ref, offset_ref):
    total = got_ref[pl.ds(0, BLOCK_OUT), :]
    for d in range(1, N_DEST):
        total = total + got_ref[pl.ds(d * BLOCK_OUT, BLOCK_OUT), :]
    late = join_thirds([total[EXTRA_OUT * third : EXTRA_OUT * (third + 1)] for third in range(3)])
    early = BLOCK_OUT - N_FIELD
    for p in range(N_SPACE):
        share_ref[pl.ds(p * SHARE, early), :] = total[N_FIELD:BLOCK_OUT]
        share_ref[pl.ds(p * SHARE + early, SHARE - early), :] = late[: SHARE - early]
    offset_ref[...] = late[SHARE - early : EXTRA_OUT]


def after_kernel(got_ref, g_ref, pair_ref, out_ref):
    for j in range(ROWS // 2):
        rows = []
        for rr in range(2):
            for of in range(2):
                for c in range(COLS):
                    rows.append(got_ref[pl.ds(slot(of, c, 2 * j + rr), N_DEST, stride=BLOCK_OUT), :])
        spectrum = halves(jnp.concatenate(rows, axis=0))
        back = product(spectrum, [pair_ref[n] for n in range(2)], TN)
        lanes = pl.ds(2 * W * j, 2 * W)
        out_ref[:, lanes] = g_ref[:, lanes] + back[:CH]


def vmem(count):
    return [pl.BlockSpec(memory_space=pltpu.VMEM)] * count


PARAMS = pltpu.CompilerParams(vmem_limit_bytes=VMEM_LIMIT)


def shards(acts, cotangent, w_in, w_out, b_in, b_out):
    everyone = ("segment", "space")
    block_input, given = acts[0, 0], cotangent[0]

    by_owner = width_table().reshape(2, COLS, N_SEG, N_SPACE, W).transpose(2, 0, 1, 3, 4)
    width_parts = split_table(by_owner.reshape(N_SEG, 2 * COLS * N_SPACE, W), 3)
    width_terms = lay_out(width_parts, 3, WIDE)
    pair_parts = split_table(row_pair_table(), 2)
    height_parts = split_table(height_table(), 3)
    height_terms = [lay_out(height_parts, parts, 2 * H) for parts in (3, 2)]

    given_arrays = (block_input, given, b_in[0], b_out[0], w_in[0, :, 0], w_out[0, :, 0], width_terms)
    copied = [(CH, ROWS * W + LANES), (CH, ROWS * W + LANES), (2, CH), (2, CH), (4, CH, CH)]
    sent = pl.pallas_call(
        ahead_kernel,
        out_shape=jax.ShapeDtypeStruct((N_DEST * BLOCK_IN, LANES), F32),
        in_specs=[pl.BlockSpec(memory_space=pl.ANY)] * len(given_arrays),
        out_specs=pl.BlockSpec(memory_space=pl.ANY),
        scratch_shapes=[pltpu.VMEM(shape, F32) for shape in copied]
        + [
            pltpu.VMEM(width_terms.shape, BF16),
            pltpu.VMEM((N_DEST * BLOCK_IN, LANES), F32),
            pltpu.SemaphoreType.DMA((1 + ROWS + 4 + N_SEG,)),
        ],
        compiler_params=pltpu.CompilerParams(vmem_limit_bytes=AHEAD_VMEM),
        name="ahead",
    )(*given_arrays)
    got = lax.all_to_all(sent.reshape(N_DEST, BLOCK_IN, 1, LANES), everyone, 0, 0, tiled=True)

    own_w = jnp.concatenate([w_in[0, :, 0], w_out[0, :, 0]])
    own_w = jnp.pad(own_w, ((0, 0), (0, 0), (0, LANES - CH))).reshape(4 * CH, LANES)
    own_b = jnp.pad(jnp.concatenate([b_in[0], b_out[0]]), ((0, 4), (0, LANES - CH)))

    sent = pl.pallas_call(
        middle_kernel,
        out_shape=jax.ShapeDtypeStruct((N_DEST * BLOCK_OUT, LANES), F32),
        in_specs=vmem(5),
        out_specs=pl.BlockSpec(memory_space=pltpu.VMEM),
        scratch_shapes=[
            pltpu.VMEM((4 * CH, LANES), F32),
            pltpu.VMEM((N_SEG * 4 * CH, LANES), F32),
            pltpu.VMEM((N_SEG, 8, LANES), F32),
        ],
        compiler_params=PARAMS,
        name="middle",
    )(got.reshape(N_DEST * BLOCK_IN, LANES), own_w, own_b, *height_terms)
    got = lax.all_to_all(sent.reshape(N_DEST, BLOCK_OUT, LANES), everyone, 0, 0, tiled=True)
    got = got.reshape(N_DEST * BLOCK_OUT, LANES)

    mine, offsets = pl.pallas_call(
        total_kernel,
        out_shape=(
            jax.ShapeDtypeStruct((N_SPACE * SHARE, LANES), F32),
            jax.ShapeDtypeStruct((4, LANES), F32),
        ),
        in_specs=vmem(1),
        out_specs=tuple(vmem(2)),
        compiler_params=PARAMS,
        name="total",
    )(got)
    whole = lax.all_to_all(mine.reshape(N_SPACE, SHARE, LANES), "space", 0, 0, tiled=True)

    adjoint = pl.pallas_call(
        after_kernel,
        out_shape=jax.ShapeDtypeStruct((CH, ROWS * W), F32),
        in_specs=vmem(3),
        out_specs=pl.BlockSpec(memory_space=pltpu.VMEM),
        compiler_params=PARAMS,
        name="after",
    )(got, given, pair_parts)

    whole = whole.reshape(4, CH, LANES)[:, :, :CH]
    offsets = offsets[:, :CH]
    return (
        adjoint[None, None],
        whole[:2].reshape(w_in.shape),
        whole[2:].reshape(w_out.shape),
        offsets[:2].reshape(b_in.shape),
        offsets[2:].reshape(b_out.shape),
    )


def solution(mesh):
    placed = (
        P("segment", None, "chan", "space"),
        P(None, "chan", "space"),
        P("segment", None, "chan", None, None),
        P("segment", None, "chan", None, None),
        P("segment", None, "chan"),
        P("segment", None, "chan"),
    )
    return jax.shard_map(
        shards,
        mesh=mesh,
        in_specs=placed,
        out_specs=(
            P("segment", None, "chan", "space"),
            P("segment", None, "chan", None, None),
            P("segment", None, "chan", None, None),
            P("segment", None, "chan"),
            P("segment", None, "chan"),
        ),
        check_vma=False,
    )
```

```python
import math

import jax
import jax.numpy as jnp
import ml_dtypes
import numpy as np
from jax import lax
from jax.experimental import pallas as pl
from jax.experimental.pallas import tpu as pltpu
from jax.sharding import PartitionSpec as P

H = 96
W = 192
CH = 96
LANES = 128
N_SPACE = 16
N_SEG = 2
N_DEST = N_SPACE * N_SEG
ROWS = H // N_SPACE
COLS = W // 2 // N_DEST
BLOCK_IN, EXTRA_IN = 51, 17
BLOCK_OUT, EXTRA_OUT = 48, 16
SHRINK = 0.3
WIDE = 256
BF16 = jnp.bfloat16
F32 = jnp.float32
VMEM_LIMIT = 24 * 1024 * 1024
AHEAD_VMEM = 56 * 1024 * 1024


def split_table(table, count):
    parts = []
    for _ in range(count):
        parts.append(table.astype(np.float32).astype(ml_dtypes.bfloat16))
        table = table - parts[-1].astype(np.float64)
    return np.stack(parts)


def dft(length):
    index = np.arange(length)
    phase = 2.0 * math.pi * (np.outer(index, index) % length) / length
    return np.cos(phase) / math.sqrt(length), np.sin(phase) / math.sqrt(length)


def width_table():
    cos_w, sin_w = dft(W)
    half = W // 2
    real, imag = cos_w[:half].copy(), -sin_w[:half].copy()
    imag[0] = cos_w[half]
    both = np.stack([real, imag])
    return both.reshape(2, N_DEST, COLS, W).transpose(0, 2, 1, 3)


def height_table():
    cos_h, sin_h = dft(H)
    order = np.array([ROWS * p + r for r in range(ROWS) for p in range(N_SPACE)])
    cos_h, sin_h = cos_h[np.ix_(order, order)], sin_h[np.ix_(order, order)]
    return np.block([[cos_h, sin_h], [-sin_h, cos_h]])


def row_pair_table():
    flat = width_table().reshape(2 * COLS * N_DEST, W)
    zero = np.zeros_like(flat)
    return np.block([[flat, zero], [zero, flat]])


def cut(value, count):
    parts = []
    for n in range(count):
        parts.append(value.astype(BF16))
        if n < count - 1:
            value = value - parts[-1].astype(F32)
    return parts


def halves(value):
    return cut(value, 2)


def thirds(value):
    return cut(value, 3)


def terms(parts):
    return [(n, order - n) for order in reversed(range(parts)) for n in range(order + 1)]


def product(a, b, contract, parts=2):
    (left,), (right,) = contract
    if isinstance(a, list):
        a = jnp.concatenate([a[n] for n, _ in terms(parts)], axis=left)
    b = jnp.concatenate([b[n] for _, n in terms(parts)], axis=right)
    return lax.dot_general(a, b, (contract, ((), ())), preferred_element_type=F32)


def lay_out(split, parts, width):
    pad = [(0, 0)] * (split.ndim - 2) + [(0, width - split.shape[-1])]
    return np.concatenate([np.pad(split[n], pad) for n, _ in terms(parts)], axis=-1)


NN = ((1,), (0,))
NT = ((1,), (1,))
TN = ((0,), (0,))


def lane_index(rows):
    return lax.broadcasted_iota(jnp.int32, (rows, LANES), 1)


def slot(part, c, r):
    return (part * COLS + c) * ROWS + r


N_FIELD = 2 * COLS * ROWS
OWN = 32
OFFSET_ROW = 2 * N_FIELD - OWN
WEIGHT_ROW = OFFSET_ROW + 4
SHARE = 4 * CH // N_SPACE


def pack_rows(put, count, values, block, extras):
    lane = lane_index(count)
    for q in range(block):
        third, extra = divmod(q, extras)
        value = values[q]
        if third < 3:
            value = jnp.where(lane < CH, value, pltpu.roll(values[block + extra], CH - 32 * third, 1))
        put(q, value)


def join_thirds(thirds_of):
    lane = lane_index(thirds_of[0].shape[0])
    value = jnp.zeros(thirds_of[0].shape, F32)
    for third, part in enumerate(thirds_of):
        moved = pltpu.roll(part, (32 * third - CH) % LANES, 1)
        value = jnp.where((lane >= 32 * third) & (lane < 32 * third + 32), moved, value)
    return value


def unpack_row(get, q, block, extras):
    if q < block:
        return get(q)
    return join_thirds([get(q - block + extras * third) for third in range(3)])


def ahead_kernel(
    x_hbm, g_hbm, b_in_hbm, b_out_hbm, w_in_hbm, w_out_hbm, table_hbm,
    out_hbm, x_ref, g_ref, b_in_ref, b_out_ref, w_ref, table_ref, out_ref, sems,
):
    segment, space = lax.axis_index("segment"), lax.axis_index("space")
    pairs = [(table_hbm, table_ref)]
    for src, dst in ((x_hbm, x_ref), (g_hbm, g_ref)):
        dst[:, pl.ds(ROWS * W, LANES)] = jnp.zeros((CH, LANES), F32)
        for j in range(ROWS // 2):
            lanes = pl.ds(2 * W * j, 2 * W)
            pairs.append((src.at[:, lanes], dst.at[:, lanes]))
    pairs += [(b_in_hbm, b_in_ref), (b_out_hbm, b_out_ref), (w_in_hbm, w_ref.at[0:2]), (w_out_hbm, w_ref.at[2:4])]
    copies = [pltpu.make_async_copy(src, dst, sems.at[n]) for n, (src, dst) in enumerate(pairs)]
    for copy in copies:
        copy.start()
    pad = jnp.zeros((LANES - CH, WIDE), F32)
    fields = [{} for _ in range(N_SEG)]
    adjoints = {}

    def all_rows(ref):
        return jnp.concatenate(
            [piece for r in range(ROWS) for piece in (ref[:, pl.ds(W * r, WIDE)], pad)], axis=0
        )

    def cut_out(value, base, r):
        return value[base : base + N_SPACE, LANES * r : LANES * (r + 1)]

    copies[0].wait()
    table = [table_ref[n].reshape(N_SEG * 2 * COLS * N_SPACE, WIDE) for n in range(3)]
    last = (2 * COLS - 1) * N_SPACE
    part = [
        jnp.concatenate([table_ref[n, segment], table_ref[n, 1 - segment, last:, :]], axis=0) for n in range(2)
    ]
    others = {}
    for copy in copies[1 : 1 + ROWS // 2]:
        copy.wait()
    field = product(table, thirds(all_rows(x_ref)), NT, 3)
    for copy in copies[1 + ROWS // 2 : 1 + ROWS]:
        copy.wait()
    adjoint = product(part, halves(all_rows(g_ref)), NT)
    for r in range(ROWS):
        for of in range(2):
            for c in range(COLS):
                at = slot(of, c, r)
                for s in range(N_SEG):
                    fields[s][at] = cut_out(field, ((s * 2 + of) * COLS + c) * N_SPACE, r)
                if at < OWN:
                    adjoints[N_FIELD + at] = cut_out(adjoint, (of * COLS + c) * N_SPACE, r)
                else:
                    others[N_FIELD + at - OWN] = cut_out(adjoint, last + N_SPACE, r)
    for copy in copies[1 + ROWS :]:
        copy.wait()

    def to_all(row):
        return jnp.broadcast_to(row, (N_SPACE, LANES))

    fill = jnp.zeros((1, LANES - CH), F32)
    for n, ref in enumerate((b_in_ref, b_out_ref)):
        for of in range(2):
            others[OFFSET_ROW + 2 * n + of] = to_all(jnp.concatenate([ref[of : of + 1, :], fill], axis=1))
    start = pl.multiple_of(lax.rem(space, 4) * SHARE, 8)
    weights = w_ref[space // 4, pl.ds(start, SHARE), :]
    weights = jnp.concatenate([weights, jnp.zeros((SHARE, LANES - CH), F32)], axis=1)
    for j in range(SHARE):
        others[WEIGHT_ROW + j] = to_all(weights[j : j + 1])

    sends = []
    for s in range(N_SEG):
        values = dict(fields[s])
        for q in range(N_FIELD, N_FIELD + OWN):
            values[q] = jnp.where(segment == s, adjoints[q], others[q])

        def put(q, value, s=s):
            out_ref[pl.ds(s * N_SPACE * BLOCK_IN + q, N_SPACE, stride=BLOCK_IN), :] = value

        pack_rows(put, N_SPACE, values, BLOCK_IN, EXTRA_IN)
        half = pl.ds(s * N_SPACE * BLOCK_IN, N_SPACE * BLOCK_IN)
        sends.append(pltpu.make_async_copy(out_ref.at[half], out_hbm.at[half], sems.at[len(copies) + s]))
        sends[-1].start()
    for send in sends:
        send.wait()


def middle_kernel(got_ref, own_w_ref, own_b_ref, long_ref, short_ref, out_ref, grads_ref, w_ref, b_ref):
    segment, space = lax.axis_index("segment"), lax.axis_index("space")
    is_special = (segment == 0) & (space == 0)
    scale = jnp.where(is_special, 1.0, 0.5).astype(F32)

    def row(source, q):
        def get(at):
            return got_ref[pl.ds(source * N_SPACE * BLOCK_IN + at, N_SPACE, stride=BLOCK_IN), :]

        return unpack_row(get, q, BLOCK_IN, EXTRA_IN)

    def field_column(s, c):
        return jnp.concatenate([row(s, slot(of, c, r)) for of in range(2) for r in range(ROWS)], axis=0)

    other = 1 - segment

    def adjoint_row(at):
        return row(segment, N_FIELD + at) if at < OWN else row(other, N_FIELD + at - OWN)

    def adjoint_column(c):
        return jnp.concatenate([adjoint_row(slot(of, c, r)) for of in range(2) for r in range(ROWS)], axis=0)

    w_ref[pl.ds(pl.multiple_of(segment * 4 * CH, 8), 4 * CH), :] = own_w_ref[...]
    b_ref[segment] = own_b_ref[...]
    inside = lane_index(N_SPACE) < CH
    for n in range(4):
        b_ref[other, n : n + 1, :] = row(other, OFFSET_ROW + n)[:1]
    for j in range(SHARE):
        w_ref[pl.ds(other * 4 * CH + j, N_SPACE, stride=SHARE), :] = jnp.where(inside, row(other, WEIGHT_ROW + j), 0.0)

    nothing = jnp.zeros((H, LANES), F32)

    def block(value, n):
        return value[:, LANES * n : LANES * (n + 1)]

    def spread(first):
        one = jnp.concatenate([first[:H], jnp.where(is_special, nothing, first[H:])], axis=0)
        return [one, jnp.concatenate([first[H:], nothing], axis=0)]

    def ordinary(column):
        r, i = column[:H], column[H:]
        return [jnp.concatenate([r, i], axis=1), jnp.concatenate([r, -i], axis=1)]

    def leading(one, two):
        mirror = jnp.where(is_special, two, jnp.concatenate([one[:H], -one[H:]], axis=0))
        return [jnp.concatenate([v[:H], v[H:]], axis=1) for v in (one, mirror)]

    def transform(columns, parts):
        table = long_ref[...] if parts == 3 else short_ref[...]
        return product(table, cut(jnp.concatenate(columns, axis=1), parts), NN, parts)

    adjoint_first = adjoint_column(0)
    fields = transform(
        [v for s in range(2) for v in spread(field_column(s, 0)) + [field_column(s, 1), field_column(s, 2)]], 3
    )
    adjoints = transform(spread(adjoint_first) + [adjoint_column(1), adjoint_column(2)], 2)

    weights = []
    gap = jnp.zeros((LANES - CH, 2 * LANES), F32)
    for s in range(N_SEG):
        for n in range(2):
            real, imag = (w_ref[pl.ds((4 * s + 2 * n + of) * CH, CH), :] for of in range(2))
            top, bottom = jnp.concatenate([real, imag], axis=1), jnp.concatenate([-imag, real], axis=1)
            weights.append(thirds(jnp.concatenate([top, gap, bottom, gap], axis=0)))

    def offset(s, n):
        return jnp.concatenate([b_ref[s, 2 * n + of : 2 * n + of + 1, :] for of in range(2)], axis=1)

    forward = []
    for s in range(2):
        parts = [block(fields, 4 * s + n) for n in range(4)]
        x = jnp.concatenate(leading(parts[0], parts[1]) + ordinary(parts[2]) + ordinary(parts[3]), axis=0)
        x = thirds(x)
        hid = product(x, weights[2 * s], NN, 3) + offset(s, 0)
        act = thirds(jnp.maximum(hid, 0.0))
        out = product(act, weights[2 * s + 1], NN, 3) + offset(s, 1)
        forward.append((x, hid, act, out))

    def backward(s, upstream):
        x, hid, act, out = forward[s]
        grad_out = jnp.where(jnp.abs(out) > SHRINK, upstream, 0.0)
        grad_out_halves = halves(grad_out)
        grad_hid = jnp.where(hid > 0.0, product(grad_out_halves, weights[2 * s + 1], NT), 0.0)
        grad_hid_halves = halves(grad_hid)
        grad_x = product(grad_hid_halves, weights[2 * s], NT)
        pairs = []
        for n, (left, right) in enumerate(((x, grad_hid_halves), (act, grad_out_halves))):
            full = product(left, right, TN)
            grads_ref[pl.ds((2 * n) * CH, CH), :] = full[:CH, :LANES] + full[LANES : LANES + CH, LANES:]
            grads_ref[pl.ds((2 * n + 1) * CH, CH), :] = full[:CH, LANES:] - full[LANES : LANES + CH, :LANES]
        offsets = []
        for value in (grad_hid, grad_out):
            total = jnp.sum(value, axis=0, keepdims=True)
            offsets += [total[:, :LANES], total[:, LANES:]]
        sums = []
        for c in range(COLS):
            one, two = grad_x[2 * c * H : (2 * c + 1) * H], grad_x[(2 * c + 1) * H : (2 * c + 2) * H]
            sums.append((one[:, :LANES] + two[:, :LANES], one[:, LANES:] - two[:, LANES:]))
        one = jnp.concatenate(
            [
                jnp.where(is_special, grad_x[:H, :LANES], sums[0][0]),
                -jnp.where(is_special, grad_x[:H, LANES:], sums[0][1]),
            ],
            axis=0,
        )
        two = jnp.concatenate([grad_x[H : 2 * H, :LANES], -grad_x[H : 2 * H, LANES:]], axis=0)
        back = transform([one, two] + [jnp.concatenate([r, -i], axis=0) for r, i in sums[1:]], 2)
        columns = []
        for n in (0, 2, 3):
            low = -block(back, n)[H:]
            if n == 0:
                low = jnp.where(is_special, block(back, 1)[:H], low)
            columns.append(jnp.concatenate([block(back, n)[:H], low], axis=0))
        return columns, [jnp.concatenate(pair, axis=0) for pair in sums[1:]], offsets

    def emit(s, columns, offsets):
        values = {}
        for c in range(COLS):
            for of in range(2):
                for r in range(ROWS):
                    base = (of * ROWS + r) * N_SPACE
                    values[slot(of, c, r)] = columns[c][base : base + N_SPACE]
        for j in range(SHARE):
            values[N_FIELD + j] = grads_ref[pl.ds(j, N_SPACE, stride=SHARE), :]
        for j in range(4):
            values[N_FIELD + SHARE + j] = jnp.broadcast_to(offsets[j], (N_SPACE, LANES))

        def put(q, value):
            out_ref[pl.ds(s * N_SPACE * BLOCK_OUT + q, N_SPACE, stride=BLOCK_OUT), :] = value

        pack_rows(put, N_SPACE, values, BLOCK_OUT, EXTRA_OUT)

    parts = [block(adjoints, n) for n in range(4)]
    upstream = jnp.concatenate(leading(parts[0], parts[1]) + ordinary(parts[2]) + ordinary(parts[3]), axis=0)
    columns_one, sums, offsets = backward(1, upstream)
    emit(1, columns_one, offsets)

    lead = transform(spread(adjoint_first + scale * columns_one[0]), 2)
    upstream = jnp.concatenate(
        leading(block(lead, 0), block(lead, 1))
        + ordinary(parts[2] + 0.5 * sums[0])
        + ordinary(parts[3] + 0.5 * sums[1]),
        axis=0,
    )
    columns_zero, sums, offsets = backward(0, upstream)
    emit(0, [one + zero for one, zero in zip(columns_one, columns_zero)], offsets)


def total_kernel(got_ref, share_ref, offset_ref):
    total = got_ref[pl.ds(0, BLOCK_OUT), :]
    for d in range(1, N_DEST):
        total = total + got_ref[pl.ds(d * BLOCK_OUT, BLOCK_OUT), :]
    late = join_thirds([total[EXTRA_OUT * third : EXTRA_OUT * (third + 1)] for third in range(3)])
    early = BLOCK_OUT - N_FIELD
    for p in range(N_SPACE):
        share_ref[pl.ds(p * SHARE, early), :] = total[N_FIELD:BLOCK_OUT]
        share_ref[pl.ds(p * SHARE + early, SHARE - early), :] = late[: SHARE - early]
    offset_ref[...] = late[SHARE - early : EXTRA_OUT]


def after_kernel(got_ref, g_ref, pair_ref, out_ref):
    for j in range(ROWS // 2):
        rows = []
        for rr in range(2):
            for of in range(2):
                for c in range(COLS):
                    rows.append(got_ref[pl.ds(slot(of, c, 2 * j + rr), N_DEST, stride=BLOCK_OUT), :])
        spectrum = halves(jnp.concatenate(rows, axis=0))
        back = product(spectrum, [pair_ref[n] for n in range(2)], TN)
        lanes = pl.ds(2 * W * j, 2 * W)
        out_ref[:, lanes] = g_ref[:, lanes] + back[:CH]


def vmem(count):
    return [pl.BlockSpec(memory_space=pltpu.VMEM)] * count


PARAMS = pltpu.CompilerParams(vmem_limit_bytes=VMEM_LIMIT)


def shards(acts, cotangent, w_in, w_out, b_in, b_out):
    everyone = ("segment", "space")
    block_input, given = acts[0, 0], cotangent[0]

    by_owner = width_table().reshape(2, COLS, N_SEG, N_SPACE, W).transpose(2, 0, 1, 3, 4)
    width_parts = split_table(by_owner.reshape(N_SEG, 2 * COLS * N_SPACE, W), 3)
    width_terms = np.pad(width_parts, ((0, 0), (0, 0), (0, 0), (0, WIDE - W)))
    pair_parts = split_table(row_pair_table(), 2)
    height_parts = split_table(height_table(), 3)
    height_terms = [lay_out(height_parts, parts, 2 * H) for parts in (3, 2)]

    given_arrays = (block_input, given, b_in[0], b_out[0], w_in[0, :, 0], w_out[0, :, 0], width_terms)
    copied = [(CH, ROWS * W + LANES), (CH, ROWS * W + LANES), (2, CH), (2, CH), (4, CH, CH)]
    sent = pl.pallas_call(
        ahead_kernel,
        out_shape=jax.ShapeDtypeStruct((N_DEST * BLOCK_IN, LANES), F32),
        in_specs=[pl.BlockSpec(memory_space=pl.ANY)] * len(given_arrays),
        out_specs=pl.BlockSpec(memory_space=pl.ANY),
        scratch_shapes=[pltpu.VMEM(shape, F32) for shape in copied]
        + [
            pltpu.VMEM(width_terms.shape, BF16),
            pltpu.VMEM((N_DEST * BLOCK_IN, LANES), F32),
            pltpu.SemaphoreType.DMA((1 + ROWS + 4 + N_SEG,)),
        ],
        compiler_params=pltpu.CompilerParams(vmem_limit_bytes=AHEAD_VMEM),
        name="ahead",
    )(*given_arrays)
    got = lax.all_to_all(sent.reshape(N_DEST, BLOCK_IN, 1, LANES), everyone, 0, 0, tiled=True)

    own_w = jnp.concatenate([w_in[0, :, 0], w_out[0, :, 0]])
    own_w = jnp.pad(own_w, ((0, 0), (0, 0), (0, LANES - CH))).reshape(4 * CH, LANES)
    own_b = jnp.pad(jnp.concatenate([b_in[0], b_out[0]]), ((0, 4), (0, LANES - CH)))

    sent = pl.pallas_call(
        middle_kernel,
        out_shape=jax.ShapeDtypeStruct((N_DEST * BLOCK_OUT, LANES), F32),
        in_specs=vmem(5),
        out_specs=pl.BlockSpec(memory_space=pltpu.VMEM),
        scratch_shapes=[
            pltpu.VMEM((4 * CH, LANES), F32),
            pltpu.VMEM((N_SEG * 4 * CH, LANES), F32),
            pltpu.VMEM((N_SEG, 8, LANES), F32),
        ],
        compiler_params=PARAMS,
        name="middle",
    )(got.reshape(N_DEST * BLOCK_IN, LANES), own_w, own_b, *height_terms)
    got = lax.all_to_all(sent.reshape(N_DEST, BLOCK_OUT, LANES), everyone, 0, 0, tiled=True)
    got = got.reshape(N_DEST * BLOCK_OUT, LANES)

    mine, offsets = pl.pallas_call(
        total_kernel,
        out_shape=(
            jax.ShapeDtypeStruct((N_SPACE * SHARE, LANES), F32),
            jax.ShapeDtypeStruct((4, LANES), F32),
        ),
        in_specs=vmem(1),
        out_specs=tuple(vmem(2)),
        compiler_params=PARAMS,
        name="total",
    )(got)
    whole = lax.all_to_all(mine.reshape(N_SPACE, SHARE, LANES), "space", 0, 0, tiled=True)

    adjoint = pl.pallas_call(
        after_kernel,
        out_shape=jax.ShapeDtypeStruct((CH, ROWS * W), F32),
        in_specs=vmem(3),
        out_specs=pl.BlockSpec(memory_space=pltpu.VMEM),
        compiler_params=PARAMS,
        name="after",
    )(got, given, pair_parts)

    whole = whole.reshape(4, CH, LANES)[:, :, :CH]
    offsets = offsets[:, :CH]
    return (
        adjoint[None, None],
        whole[:2].reshape(w_in.shape),
        whole[2:].reshape(w_out.shape),
        offsets[:2].reshape(b_in.shape),
        offsets[2:].reshape(b_out.shape),
    )


def solution(mesh):
    placed = (
        P("segment", None, "chan", "space"),
        P(None, "chan", "space"),
        P("segment", None, "chan", None, None),
        P("segment", None, "chan", None, None),
        P("segment", None, "chan"),
        P("segment", None, "chan"),
    )
    return jax.shard_map(
        shards,
        mesh=mesh,
        in_specs=placed,
        out_specs=(
            P("segment", None, "chan", "space"),
            P("segment", None, "chan", None, None),
            P("segment", None, "chan", None, None),
            P("segment", None, "chan"),
            P("segment", None, "chan"),
        ),
        check_vma=False,
    )
```
